256 devices in a mesh: seq: 32 (over x, y, core), exp: 8 (over z).
Axes of the slice: x: 4, y: 4, z: 8, core: 2. Of those that a mesh axis runs over, the one named last changes fastest.
Arguments:
- residual_in: bfloat16 [4096, 4096], P('seq', 'exp'), may hold values from -12 to 12
- queries: bfloat16 [4096, 2048], P('seq', 'exp'), may hold values from -5.5 to 5.5
- key_heads: bfloat16 [4096, 1024], P('seq', 'exp'), may hold values from -5.5 to 5.5
- value_heads: bfloat16 [4096, 1024], P('seq', 'exp'), may hold values from -6 to 6
- out_proj: bfloat16 [2048, 4096], P('exp'), may hold values from -0.25 to 0.25
- norm_gain: float32 [4096], replicated, may hold values from 0.25 to 1.75
- expert_ids: int32 [4096, 8], P('seq'), may hold values from 0 to 63, all different within a row; in each aligned block of 128 rows (0 to 127, 128 to 255, ...) at most 32 rows name the same one
- route_weights: bfloat16 [4096, 8], P('seq'), may hold values from 0.049804688 to 0.29882812
- changed: int32 [4096], P('seq'), may hold values 0 or 1
- cached_moe: bfloat16 [4096, 4096], P('seq', 'exp'), may hold values from -3 to 3
- gate_proj: bfloat16 [256, 4096, 384], P(('exp', 'seq')), may hold values from -0.09375 to 0.09375
- up_proj: bfloat16 [256, 4096, 384], P(('exp', 'seq')), may hold values from -0.09375 to 0.09375
- down_proj: bfloat16 [256, 384, 4096], P(('exp', 'seq')), may hold values from -0.15625 to 0.15625
Outputs:
- layer_out: bfloat16 [4096, 4096], P('seq', 'exp')
The draws below stay inside these ranges and needn't reach their ends.
Inputs may be any that keep to these rules, and one draw needn't show every extreme that they name: `expert_ids`: each row names 8 different experts. Among the 128 rows of one index of seq no expert is named by more than 32 rows, a bound that some block reaches.
All inputs are finite; a program needn't handle non-finite values. No bound on the sum of `changed` on one device may be relied on, other than what follows from the above.
Results may differ from the reference program's by a relative error of at most 0.014.
Values may be sent and summed in bfloat16 or wider, within the bound.
No kernel may reach another device: no remote copies, remote signals or barrier semaphores. Data moves between devices by JAX's collectives and lax.ppermute only.
A program may use at most 128 MiB of HBM per device.

```python
import math
import jax
import jax.numpy as jnp
import numpy as np
from jax import lax

D = 4096
FW = 1536
HQ = 16
HK = 8
HD = 128
TOP = 8
T_SEQ = 128
LENGTH = 4096
EXPERTS = 64
SPLITS = 4
FS = 384
CAP = 32
N_SEQ = 32


def draw_queries(key, part):
    key = jax.random.fold_in(key, 11)
    base = jnp.clip(1.5 * jax.random.normal(key, (LENGTH, HQ * HD), jnp.float32), -5.5, 5.5)
    return base.astype(jnp.bfloat16)


def draw_key_heads(key, part):
    key = jax.random.fold_in(key, 12)
    base = jnp.clip(1.5 * jax.random.normal(key, (LENGTH, HK * HD), jnp.float32), -5.5, 5.5)
    return base.astype(jnp.bfloat16)


def draw_residual_in(key, part):
    key = jax.random.fold_in(key, 13)
    row_key, col_key, value_key = jax.random.split(key, 3)
    row_scale = jnp.exp(jax.random.uniform(row_key, (LENGTH, 1), jnp.float32, math.log(0.3), math.log(3.0)))
    col_scale = jnp.exp(jax.random.uniform(col_key, (1, D), jnp.float32, math.log(0.3), math.log(3.0)))
    values = jax.random.normal(value_key, (LENGTH, D), jnp.float32)
    return jnp.clip(values * row_scale * col_scale, -12.0, 12.0).astype(jnp.bfloat16)


def plant(array, key, low, high):
    shape = array.shape
    place = [jax.random.randint(jax.random.fold_in(key, axis), (), 0, shape[axis]) for axis in range(len(shape))]
    array = array.at[tuple(place)].set(low)
    longest = shape.index(max(shape))
    place[longest] = (place[longest] + 1) % shape[longest]
    return array.at[tuple(place)].set(high)


def levels(own_key, shape, cuts, least, top_value):
    gain = 1.0
    for position, shards_of in cuts:
        steps = jax.random.uniform(jax.random.fold_in(jax.random.fold_in(own_key, 6), position), (shards_of,), jnp.float32, least / len(cuts), top_value / len(cuts))
        gain = gain * jnp.repeat(jnp.exp(steps), shape[position] // shards_of).reshape((-1,) + (1,) * (len(shape) - 1 - position))
    return gain


def assign_block(rng, own, number, rows, count, top, bound, lean):
    order = jax.random.permutation(rng, count)
    packed, usual = load_shares(count, rows * top, bound, lean, True), load_shares(count, rows * top, bound, lean, False)
    places = jnp.arange(count)

    def named(tallies, rotation):
        used = int((tallies > 0).sum())
        fixed = max(1, used // 4)
        shifted = fixed + (places - fixed + rotation * (used - fixed)) % max(1, count - fixed)
        return jnp.zeros((count,), jnp.int32).at[order[jnp.where(places < fixed, places, shifted)]].set(jnp.asarray(tallies, jnp.int32))

    tallies = jnp.where(number % 4 == 0, named(packed, number // 4), named(usual, number - number // 4 - 1))
    mixed = jax.random.permutation(jax.random.fold_in(own, 3), count)
    donor, receiver = mixed[0:count // 2 * 2:2], mixed[1:count // 2 * 2:2]
    room = jnp.minimum(tallies[donor] - 1, bound - tallies[receiver]) // 2
    room = jnp.where((donor == order[0]) | (receiver == order[0]) | (tallies[receiver] == 0), 0, jnp.maximum(room, 0))
    shifted = jax.random.randint(jax.random.fold_in(own, 4), (count // 2,), 0, 1 << 20) % (room + 1)
    tallies = tallies.at[donor].add(-shifted).at[receiver].add(shifted)
    labels = jnp.searchsorted(jnp.cumsum(tallies), jnp.arange(rows * top), side="right").astype(jnp.int32)
    grid = labels.reshape(top, rows).T
    grid = grid[jax.random.permutation(jax.random.fold_in(own, 1), rows)]
    rotation = jax.random.randint(jax.random.fold_in(own, 2), (rows, 1), 0, top)
    return jnp.take_along_axis(grid, (jnp.arange(top)[None, :] + rotation) % top, axis=1)


def load_shares(number_of, total, most, lean, full):
    portions = [(1 << 20) // math.isqrt(rank ** lean) + 1 for rank in range(1, number_of + 1)]
    largest = most if full else min(most, max(-(-total // number_of), total * portions[0] // sum(portions)))
    least = 1 if total - largest >= number_of - 1 else 0
    counts, spare = [largest] + [least] * (number_of - 1), total - largest - least * (number_of - 1)
    while spare > 0:
        free = [i for i in range(1, number_of) if counts[i] < largest] or [i for i in range(1, number_of) if counts[i] < most]
        pool, remaining = sum([portions[i] for i in free]), spare
        for i in free:
            more = min(most - counts[i], max(1, remaining * portions[i] // pool), spare)
            counts[i] = counts[i] + more
            spare = spare - more
    return np.array(counts)


def normal_values(key, dims, spread, bound, cuts=(), kind=jnp.bfloat16):
    factor_of = levels(key, dims, cuts, -0.22, 0.18) if cuts else 1.0
    entries = jax.random.normal(key, dims, jnp.float32) * spread * factor_of
    return jnp.minimum(jnp.maximum(entries, -bound), bound).astype(kind)


def setup_inputs(seed: int = 0) -> dict:
    key_of = jax.random.split(jax.random.key(seed), 14)
    residual_in = draw_residual_in(jax.random.fold_in(key_of[13], 71), 0)
    queries = draw_queries(jax.random.fold_in(key_of[13], 71), 0)
    key_heads = draw_key_heads(jax.random.fold_in(key_of[13], 71), 0)
    value_heads = normal_values(key_of[3], (LENGTH, HK * HD), 1.0, 6.0, ((0, 32), (1, 8)))
    out_proj = normal_values(key_of[4], (HQ * HD, D), (HQ * HD // 4) ** -0.5, 0.25, ((0, 8),))
    norm_gain = jnp.clip(1.0 + 0.15 * jax.random.normal(key_of[5], (D,), jnp.float32), 0.25, 1.75)
    expert_ids_keys = jax.random.split(jax.random.fold_in(key_of[6], 1), LENGTH // T_SEQ)
    expert_ids_turns = jax.random.permutation(jax.random.fold_in(key_of[6], 3), LENGTH // T_SEQ)
    expert_ids = jax.vmap(lambda own, number: assign_block(jax.random.fold_in(key_of[6], 2), own, number, T_SEQ, EXPERTS, TOP, CAP, 2))(expert_ids_keys, expert_ids_turns).reshape((LENGTH, TOP))
    route_weights = jnp.clip(0.049804688 + 0.24902344 * jax.random.uniform(key_of[7], (LENGTH, TOP), jnp.float32) ** levels(key_of[7], (LENGTH, TOP), ((0, 32),), -0.2, 0.2), 0.049804688, 0.29882812).astype(jnp.bfloat16)
    changed = plant((jax.random.randint(key_of[8], (LENGTH,), 0, 4) < 3).astype(jnp.int32), jax.random.fold_in(key_of[8], 1), 0, 1)
    cached_moe = normal_values(key_of[9], (LENGTH, D), 0.5, 3.0, ((0, 32), (1, 8)))
    gate_proj = normal_values(key_of[10], (EXPERTS * SPLITS, D, FS), D ** -0.5, 0.09375, ((0, 256),))
    up_proj = normal_values(key_of[11], (EXPERTS * SPLITS, D, FS), D ** -0.5, 0.09375, ((0, 256),))
    down_proj = normal_values(key_of[12], (EXPERTS * SPLITS, FS, D), FW ** -0.5, 0.15625, ((0, 256),))
    return {"residual_in": residual_in, "queries": queries, "key_heads": key_heads, "value_heads": value_heads, "out_proj": out_proj, "norm_gain": norm_gain, "expert_ids": expert_ids, "route_weights": route_weights, "changed": changed, "cached_moe": cached_moe, "gate_proj": gate_proj, "up_proj": up_proj, "down_proj": down_proj}


def attend(queries, key_heads, value_heads):
    group_size = HQ // HK
    query_all = queries.reshape(LENGTH, HK, group_size, HD).transpose(1, 0, 2, 3)
    key_all = key_heads.reshape(LENGTH, HK, HD).transpose(1, 0, 2)
    value_all = value_heads.reshape(LENGTH, HK, HD).transpose(1, 0, 2)

    def one_head(operands):
        query_part, key_part, value_part = operands
        scores = jnp.einsum('tgd,sd->gts', query_part.astype(jnp.float32), key_part.astype(jnp.float32)) * HD ** (-0.5)
        attn_probs = jax.nn.softmax(scores, axis=-1).astype(jnp.bfloat16)
        result = jnp.einsum('gts,sd->tgd', attn_probs.astype(jnp.float32), value_part.astype(jnp.float32))
        return result.astype(jnp.bfloat16)
    outputs = lax.map(one_head, (query_all, key_all, value_all))
    return outputs.transpose(1, 0, 2, 3).reshape(LENGTH, HQ * HD)

def reference(residual_in, queries, key_heads, value_heads, out_proj, norm_gain, expert_ids, route_weights, changed, cached_moe, gate_proj, up_proj, down_proj):
    attended = attend(queries, key_heads, value_heads)
    attn = jnp.dot(attended, out_proj, preferred_element_type=jnp.float32)
    mixed_full = (residual_in.astype(jnp.float32) + attn).astype(jnp.bfloat16)
    mixed_float = mixed_full.astype(jnp.float32)
    mean_square = lax.optimization_barrier(jnp.mean(mixed_float * mixed_float, axis=-1, keepdims=True))
    normed = (mixed_float * lax.rsqrt(mean_square + 1e-06) * norm_gain).astype(jnp.bfloat16)
    expert_range = jnp.arange(EXPERTS, dtype=jnp.int32)
    matches = expert_ids[:, :, None] == expert_range[None, None, :]
    member = jnp.any(matches, axis=1)
    token_weight = lax.optimization_barrier(jnp.sum(jnp.where(matches, route_weights.astype(jnp.float32)[:, :, None], jnp.zeros((), jnp.float32)), axis=1))
    block_member = member.reshape(N_SEQ, T_SEQ, EXPERTS).astype(jnp.int32)
    rank = jnp.cumsum(block_member, axis=1) - 1
    block_index = jnp.broadcast_to(jnp.arange(N_SEQ, dtype=jnp.int32)[:, None, None], rank.shape)
    expert_index = jnp.broadcast_to(expert_range[None, None, :], rank.shape)
    token_index = jnp.broadcast_to(jnp.arange(LENGTH, dtype=jnp.int32).reshape(N_SEQ, T_SEQ, 1), rank.shape)
    slot_index = jnp.where(block_member == 1, rank, CAP).astype(jnp.int32)
    table = jnp.zeros((N_SEQ, EXPERTS, CAP), jnp.int32).at[block_index, expert_index, slot_index].set(token_index, mode='drop')
    filled = jnp.zeros((N_SEQ, EXPERTS, CAP), jnp.float32).at[block_index, expert_index, slot_index].set(1.0, mode='drop')
    table = table.transpose(1, 0, 2).reshape(EXPERTS, N_SEQ * CAP)
    filled = filled.transpose(1, 0, 2).reshape(EXPERTS, N_SEQ * CAP)
    gate_all = gate_proj.reshape(EXPERTS, SPLITS, D, FS)
    up_all = up_proj.reshape(EXPERTS, SPLITS, D, FS)
    down_all = down_proj.reshape(EXPERTS, SPLITS, FS, D)

    def one_expert(moe_new, operands):
        slot_tokens, slot_valid, gate_part, up_part, down_part, weight_col = operands
        rows_in = normed[slot_tokens].astype(jnp.float32)
        gate_out = jnp.einsum('rd,jdf->jrf', rows_in, gate_part.astype(jnp.float32))
        up_out = jnp.einsum('rd,jdf->jrf', rows_in, up_part.astype(jnp.float32))
        hidden = (jax.nn.silu(gate_out) * up_out).astype(jnp.bfloat16)
        partial_out = jnp.einsum('jrf,jfd->jrd', hidden.astype(jnp.float32), down_part.astype(jnp.float32)).astype(jnp.bfloat16)
        expert_out = lax.optimization_barrier(jnp.sum(partial_out.astype(jnp.float32), axis=0)).astype(jnp.bfloat16)
        row_scale = weight_col[slot_tokens] * slot_valid
        return (moe_new.at[slot_tokens].add(expert_out.astype(jnp.float32) * row_scale[:, None]), None)
    moe_new, unused = lax.scan(one_expert, jnp.zeros((LENGTH, D), jnp.float32), (table, filled, gate_all, up_all, down_all, token_weight.T))
    moe_value = jnp.where(changed[:, None] == 1, moe_new, cached_moe.astype(jnp.float32))
    return (mixed_float + moe_value).astype(jnp.bfloat16)
```

```python
import jax
import jax.numpy as jnp
from jax import lax
from jax.sharding import Mesh, PartitionSpec as P

HD = 128
TOP = 8
EXP_GROUP = 8
BF = jnp.bfloat16
F32 = jnp.float32


def swap_cores(array):
    return lax.ppermute(array, "c", [(0, 1), (1, 0)])


def gather_by_exchange(array, axes, count):
    spread = jnp.broadcast_to(array[None], (count,) + array.shape)
    return lax.all_to_all(spread, axes, split_axis=0, concat_axis=0, tiled=True)


def attention(queries, all_kv, kv_local):
    tokens = queries.shape[0]
    group_size = queries.shape[1] // HD // kv_local
    width = kv_local * HD
    query_split = queries.reshape(tokens, kv_local, group_size, HD)
    key_split = all_kv[:, :width].reshape(-1, kv_local, HD)
    value_split = all_kv[:, width:].reshape(-1, kv_local, HD)
    scores = jnp.einsum(
        "tkgd,skd->kgts", query_split, key_split, preferred_element_type=F32
    ) * HD ** (-0.5)
    attn_probs = jax.nn.softmax(scores, axis=-1).astype(BF)
    attended = jnp.einsum(
        "kgts,skd->tkgd", attn_probs, value_split, preferred_element_type=F32
    ).astype(BF)
    return attended.reshape(tokens, -1)


def shards(
    residual_in,
    queries,
    key_heads,
    value_heads,
    out_proj,
    norm_gain,
    expert_ids,
    route_weights,
    changed,
    cached_moe,
    gate_proj,
    up_proj,
    down_proj,
):
    plane = lax.axis_size("x") * lax.axis_size("y")
    depth = lax.axis_size("z")
    group_index = lax.axis_index("z")
    core = lax.axis_index("c")
    tokens = queries.shape[0]
    slice_width = residual_in.shape[1]

    own_kv = gather_by_exchange(
        jnp.concatenate([key_heads, value_heads], axis=1), ("x", "y"), plane
    )
    all_kv = jnp.concatenate([own_kv, swap_cores(own_kv)], axis=0)
    all_kv = all_kv.reshape(-1, all_kv.shape[-1])

    half_rows = out_proj.shape[0] // 2
    out_half = lax.dynamic_slice_in_dim(out_proj, core * half_rows, half_rows, 0)
    out_own = lax.all_to_all(
        out_half.reshape(half_rows, depth, slice_width).transpose(1, 0, 2),
        "z", split_axis=0, concat_axis=0, tiled=True,
    )
    out_cols = jnp.concatenate([out_own, swap_cores(out_own)], axis=1)
    out_cols = out_cols.reshape(-1, slice_width)

    gate_other, up_other, down_other = (
        swap_cores(gate_proj[0]),
        swap_cores(up_proj[0]),
        swap_cores(down_proj[0]),
    )

    attended = attention(queries, all_kv, key_heads.shape[1] // HD)
    first, second = attended[:, :half_rows], attended[:, half_rows:]
    attended = jnp.where(
        core == 0,
        attended,
        jnp.concatenate([second, first], axis=1),
    )
    attended_all = gather_by_exchange(attended, "z", depth)
    attended_all = attended_all.transpose(1, 0, 2).reshape(tokens, -1)
    attn_share = jnp.dot(attended_all, out_cols, preferred_element_type=F32)
    mixed_local = (residual_in.astype(F32) + attn_share).astype(BF)

    mixed_full = gather_by_exchange(mixed_local, "z", depth)
    mixed_full = mixed_full.transpose(1, 0, 2).reshape(tokens, -1)
    mixed_float = mixed_full.astype(F32)
    mean_square = jnp.mean(mixed_float * mixed_float, axis=-1, keepdims=True)
    normed = (mixed_float * lax.rsqrt(mean_square + 1e-06) * norm_gain).astype(BF)

    capacity = 2 * tokens * TOP // (EXP_GROUP * depth)
    copies = plane // EXP_GROUP
    local_experts = jnp.arange(EXP_GROUP, dtype=jnp.int32) + group_index * EXP_GROUP
    matches = expert_ids[:, :, None] == local_experts[None, None, :]
    member = jnp.any(matches, axis=1)
    token_weight = jnp.sum(
        jnp.where(matches, route_weights[:, :, None], jnp.zeros((), BF)), axis=1
    )
    rank = jnp.cumsum(member.astype(jnp.int32), axis=0) - 1
    live_rows = member & (changed[:, None] == 1)
    slot_range = jnp.arange(capacity, dtype=jnp.int32)
    select_hit = live_rows.T[:, None, :] & (rank.T[:, None, :] == slot_range[None, :, None])
    selector = select_hit.astype(BF)
    weighted_select = selector * token_weight.T[:, None, :]
    selector = jnp.repeat(selector, copies, axis=0)
    weighted_select = jnp.repeat(weighted_select, copies, axis=0)

    outgoing = jnp.einsum(
        "jct,td->jcd", selector, normed, preferred_element_type=F32
    ).astype(BF)
    arrived = lax.all_to_all(outgoing, ("x", "y"), split_axis=0, concat_axis=0, tiled=True)
    rows = arrived.reshape(-1, arrived.shape[-1])

    def hidden_of(gate, up):
        gate_out = jnp.dot(rows, gate, preferred_element_type=F32)
        up_out = jnp.dot(rows, up, preferred_element_type=F32)
        return (jax.nn.silu(gate_out) * up_out).astype(BF)

    hidden_own = hidden_of(gate_proj[0], up_proj[0])
    hidden_other = hidden_of(gate_other, up_other)
    partial_out = (
        jnp.dot(hidden_own, down_proj[0], preferred_element_type=F32)
        + jnp.dot(hidden_other, down_other, preferred_element_type=F32)
    ).astype(BF)
    returned = lax.all_to_all(
        partial_out.reshape(arrived.shape), ("x", "y"), split_axis=0, concat_axis=0, tiled=True
    )
    combined = jnp.einsum(
        "jct,jcd->td", weighted_select, returned, preferred_element_type=F32
    ).astype(BF)
    shares = lax.all_to_all(
        combined.reshape(tokens, depth, slice_width).transpose(1, 0, 2),
        "z", split_axis=0, concat_axis=0, tiled=True,
    )
    moe_share = jnp.sum(shares.astype(F32), axis=0)
    moe_value = jnp.where(changed[:, None] == 1, moe_share, cached_moe.astype(F32))
    return (mixed_local.astype(F32) + moe_value).astype(BF)


def solution(mesh):
    cores = 2
    side = int(round((mesh.shape["seq"] // cores) ** 0.5))
    split_mesh = Mesh(
        mesh.devices.reshape(side, side, cores, mesh.shape["exp"]), ("x", "y", "c", "z")
    )
    seq = ("x", "y", "c")
    in_specs = (
        P(seq, "z"),
        P(seq, "z"),
        P(seq, "z"),
        P(seq, "z"),
        P("z", None),
        P(),
        P(seq, None),
        P(seq, None),
        P(seq),
        P(seq, "z"),
        P(("z",) + seq, None, None),
        P(("z",) + seq, None, None),
        P(("z",) + seq, None, None),
    )
    return jax.shard_map(
        shards, mesh=split_mesh, in_specs=in_specs, out_specs=P(seq, "z"), check_vma=False
    )
```

```python
import jax
import jax.numpy as jnp
from jax import lax
from jax.experimental import pallas as pl
from jax.experimental.pallas import tpu as pltpu
from jax.sharding import Mesh, PartitionSpec as P

HD = 128
TOP = 8
EXP_GROUP = 8
BF = jnp.bfloat16
F32 = jnp.float32
STEPS = 4
PIECES = 4


def swap_cores(array):
    return lax.ppermute(array, "c", [(0, 1), (1, 0)])


def gather_by_exchange(array, axes, count):
    spread = jnp.broadcast_to(array[None], (count,) + array.shape)
    return lax.all_to_all(spread, axes, split_axis=0, concat_axis=0, tiled=True)


def expert_kernel(
    rows, gate_a, up_a, down_a, gate_b, up_b, down_b, out, totals, hidden
):
    part = gate_a.shape[1]
    deep = gate_a.shape[0] // STEPS
    width = down_a.shape[1] // PIECES
    for which, (gate, up) in enumerate(((gate_a, up_a), (gate_b, up_b))):
        for step in range(STEPS):
            here = pl.ds(step * deep, deep)
            weights = jnp.concatenate([gate[here], up[here]], axis=1)
            product = jnp.dot(rows[:, here], weights, preferred_element_type=F32)
            if step:
                product += totals[...]
            if step < STEPS - 1:
                totals[...] = product
        gate_out, up_out = product[:, :part], product[:, part:]
        hidden[:, pl.ds(which * part, part)] = (jax.nn.silu(gate_out) * up_out).astype(BF)
    for piece in range(PIECES):
        columns = pl.ds(piece * width, width)
        down = jnp.concatenate([down_a[:, columns], down_b[:, columns]], axis=0)
        out[:, columns] = jnp.dot(hidden[...], down, preferred_element_type=F32).astype(BF)


def expert_partial(rows, gate_a, up_a, down_a, gate_b, up_b, down_b):
    count, depth = rows.shape
    part = gate_a.shape[1]
    return pl.pallas_call(
        expert_kernel,
        out_shape=jax.ShapeDtypeStruct((count, depth), BF),
        in_specs=[pl.BlockSpec(memory_space=pltpu.VMEM)] * 7,
        out_specs=pl.BlockSpec(memory_space=pltpu.VMEM),
        scratch_shapes=[
            pltpu.VMEM((count, 2 * part), F32),
            pltpu.VMEM((count, 2 * part), BF),
        ],
        compiler_params=pltpu.CompilerParams(vmem_limit_bytes=16 * 2**20),
        cost_estimate=pl.CostEstimate(
            flops=12 * count * depth * part,
            bytes_accessed=12 * depth * part + 4 * count * depth,
            transcendentals=2 * count * part,
        ),
        name="expert_partial",
    )(*[
        pltpu.with_memory_space_constraint(operand, pltpu.VMEM)
        for operand in (rows, gate_a, up_a, down_a, gate_b, up_b, down_b)
    ])


def attention(queries, all_kv, kv_local):
    tokens = queries.shape[0]
    group_size = queries.shape[1] // HD // kv_local
    width = kv_local * HD
    query_split = queries.reshape(tokens, kv_local, group_size, HD)
    key_split = all_kv[:, :width].reshape(-1, kv_local, HD)
    value_split = all_kv[:, width:].reshape(-1, kv_local, HD)
    scores = jnp.einsum(
        "tkgd,skd->kgts", query_split, key_split, preferred_element_type=F32
    ) * HD ** (-0.5)
    attn_probs = jax.nn.softmax(scores, axis=-1).astype(BF)
    attended = jnp.einsum(
        "kgts,skd->tkgd", attn_probs, value_split, preferred_element_type=F32
    ).astype(BF)
    return attended.reshape(tokens, -1)


def shards(
    residual_in,
    queries,
    key_heads,
    value_heads,
    out_proj,
    norm_gain,
    expert_ids,
    route_weights,
    changed,
    cached_moe,
    gate_proj,
    up_proj,
    down_proj,
):
    plane = lax.axis_size("x") * lax.axis_size("y")
    depth = lax.axis_size("z")
    group_index = lax.axis_index("z")
    core = lax.axis_index("c")
    tokens = queries.shape[0]
    slice_width = residual_in.shape[1]

    own_kv = gather_by_exchange(
        jnp.concatenate([key_heads, value_heads], axis=1), ("x", "y"), plane
    )
    all_kv = jnp.concatenate([own_kv, swap_cores(own_kv)], axis=0)
    all_kv = all_kv.reshape(-1, all_kv.shape[-1])

    half_rows = out_proj.shape[0] // 2
    out_half = lax.dynamic_slice_in_dim(out_proj, core * half_rows, half_rows, 0)
    out_own = []
    for step in range(depth):
        target = lax.rem(group_index + depth - step, depth)
        piece = lax.dynamic_slice_in_dim(out_half, target * slice_width, slice_width, 1)
        if step:
            piece = lax.ppermute(
                piece, "z", [(i, (i + depth - step) % depth) for i in range(depth)]
            )
        out_own.append(piece)
    out_own = jnp.stack(out_own)
    out_cols = jnp.concatenate([out_own, swap_cores(out_own)], axis=1)
    out_cols = out_cols.reshape(-1, slice_width)

    gate_other, up_other, down_other = (
        swap_cores(gate_proj[0]),
        swap_cores(up_proj[0]),
        swap_cores(down_proj[0]),
    )

    attended = attention(queries, all_kv, key_heads.shape[1] // HD)
    first, second = attended[:, :half_rows], attended[:, half_rows:]
    attended = jnp.where(
        core == 0,
        attended,
        jnp.concatenate([second, first], axis=1),
    )
    attended_all = gather_by_exchange(attended, "z", depth)
    attended_all = lax.dynamic_slice_in_dim(
        jnp.concatenate([attended_all, attended_all], axis=0), group_index, depth, 0
    )
    attended_all = attended_all.transpose(1, 0, 2).reshape(tokens, -1)
    attn_share = jnp.dot(attended_all, out_cols, preferred_element_type=F32)
    mixed_local = (residual_in.astype(F32) + attn_share).astype(BF)

    mixed_full = gather_by_exchange(mixed_local, "z", depth)
    mixed_full = mixed_full.transpose(1, 0, 2).reshape(tokens, -1)
    mixed_float = mixed_full.astype(F32)
    mean_square = jnp.mean(mixed_float * mixed_float, axis=-1, keepdims=True)
    normed = (mixed_float * lax.rsqrt(mean_square + 1e-06) * norm_gain).astype(BF)

    capacity = 2 * tokens * TOP // (EXP_GROUP * depth)
    copies = plane // EXP_GROUP
    local_experts = jnp.arange(EXP_GROUP, dtype=jnp.int32) + group_index * EXP_GROUP
    matches = expert_ids[:, :, None] == local_experts[None, None, :]
    member = jnp.any(matches, axis=1)
    token_weight = jnp.sum(
        jnp.where(matches, route_weights[:, :, None], jnp.zeros((), BF)), axis=1
    )
    rank = jnp.cumsum(member.astype(jnp.int32), axis=0) - 1
    live_rows = member & (changed[:, None] == 1)
    slot_range = jnp.arange(capacity, dtype=jnp.int32)
    select_hit = live_rows.T[:, None, :] & (rank.T[:, None, :] == slot_range[None, :, None])
    selector = select_hit.astype(BF)
    weighted_select = selector * token_weight.T[:, None, :]
    selector = jnp.repeat(selector, copies, axis=0)
    weighted_select = jnp.repeat(weighted_select, copies, axis=0)

    outgoing = jnp.einsum(
        "jct,td->jcd", selector, normed, preferred_element_type=F32
    ).astype(BF)
    arrived = lax.all_to_all(outgoing, ("x", "y"), split_axis=0, concat_axis=0, tiled=True)
    rows = arrived.reshape(-1, arrived.shape[-1])

    partial_out = expert_partial(
        rows, gate_proj[0], up_proj[0], down_proj[0], gate_other, up_other, down_other
    )
    returned = lax.all_to_all(
        partial_out.reshape(arrived.shape), ("x", "y"), split_axis=0, concat_axis=0, tiled=True
    )
    combined = jnp.einsum(
        "jct,jcd->td", weighted_select, returned, preferred_element_type=F32
    ).astype(BF)
    shares = lax.all_to_all(
        combined.reshape(tokens, depth, slice_width).transpose(1, 0, 2),
        "z", split_axis=0, concat_axis=0, tiled=True,
    )
    moe_share = jnp.sum(shares.astype(F32), axis=0)
    moe_value = jnp.where(changed[:, None] == 1, moe_share, cached_moe.astype(F32))
    return (mixed_local.astype(F32) + moe_value).astype(BF)


def solution(mesh):
    cores = 2
    side = int(round((mesh.shape["seq"] // cores) ** 0.5))
    split_mesh = Mesh(
        mesh.devices.reshape(side, side, cores, mesh.shape["exp"]), ("x", "y", "c", "z")
    )
    seq = ("x", "y", "c")
    in_specs = (
        P(seq, "z"),
        P(seq, "z"),
        P(seq, "z"),
        P(seq, "z"),
        P("z", None),
        P(),
        P(seq, None),
        P(seq, None),
        P(seq),
        P(seq, "z"),
        P(("z",) + seq, None, None),
        P(("z",) + seq, None, None),
        P(("z",) + seq, None, None),
    )
    return jax.shard_map(
        shards, mesh=split_mesh, in_specs=in_specs, out_specs=P(seq, "z"), check_vma=False
    )
```

```python
import jax
import jax.numpy as jnp
from jax import lax
from jax.experimental import pallas as pl
from jax.experimental.pallas import tpu as pltpu
from jax.sharding import Mesh, PartitionSpec as P

HD = 128
TOP = 8
EXP_GROUP = 8
BF = jnp.bfloat16
F32 = jnp.float32
PIECES = 4


def swap_cores(array):
    return lax.ppermute(array, "c", [(0, 1), (1, 0)])


def gather_by_exchange(array, axes, count):
    spread = jnp.broadcast_to(array[None], (count,) + array.shape)
    return lax.all_to_all(spread, axes, split_axis=0, concat_axis=0, tiled=True)


def sum_slices(array, depth):
    tokens, width = array.shape
    slices = array.reshape(tokens, depth, width // depth).transpose(1, 0, 2)
    shares = lax.all_to_all(slices, "z", split_axis=0, concat_axis=0, tiled=True)
    return jnp.sum(shares.astype(F32), axis=0)


def expert_kernel(
    rows, gate_a, up_a, down_a, gate_b, up_b, down_b, out, gate_out, hidden
):
    width = down_a.shape[1] // PIECES
    gates = jnp.concatenate([gate_a[...], gate_b[...]], axis=1)
    gate_out[...] = jnp.dot(rows[...], gates, preferred_element_type=F32)
    ups = jnp.concatenate([up_a[...], up_b[...]], axis=1)
    up_out = jnp.dot(rows[...], ups, preferred_element_type=F32)
    hidden[...] = (jax.nn.silu(gate_out[...]) * up_out).astype(BF)
    for piece in range(PIECES):
        columns = pl.ds(piece * width, width)
        down = jnp.concatenate([down_a[:, columns], down_b[:, columns]], axis=0)
        out[:, columns] = jnp.dot(hidden[...], down, preferred_element_type=F32).astype(BF)


def expert_partial(rows, gate_a, up_a, down_a, gate_b, up_b, down_b):
    count, depth = rows.shape
    part = gate_a.shape[1]
    return pl.pallas_call(
        expert_kernel,
        out_shape=jax.ShapeDtypeStruct((count, depth), BF),
        in_specs=[pl.BlockSpec(memory_space=pltpu.VMEM)] * 7,
        out_specs=pl.BlockSpec(memory_space=pltpu.VMEM),
        scratch_shapes=[
            pltpu.VMEM((count, 2 * part), F32),
            pltpu.VMEM((count, 2 * part), BF),
        ],
        compiler_params=pltpu.CompilerParams(vmem_limit_bytes=16 * 2**20),
        cost_estimate=pl.CostEstimate(
            flops=12 * count * depth * part,
            bytes_accessed=12 * depth * part + 4 * count * depth,
            transcendentals=2 * count * part,
        ),
        name="expert_partial",
    )(*[
        pltpu.with_memory_space_constraint(operand, pltpu.VMEM)
        for operand in (rows, gate_a, up_a, down_a, gate_b, up_b, down_b)
    ])


def attention(queries, all_kv, kv_local):
    tokens = queries.shape[0]
    group_size = queries.shape[1] // HD // kv_local
    width = kv_local * HD
    query_split = queries.reshape(tokens, kv_local, group_size, HD)
    key_split = all_kv[:, :width].reshape(-1, kv_local, HD)
    value_split = all_kv[:, width:].reshape(-1, kv_local, HD)
    scores = jnp.einsum(
        "tkgd,skd->kgts", query_split, key_split, preferred_element_type=F32
    ) * HD ** (-0.5)
    attn_probs = jax.nn.softmax(scores, axis=-1).astype(BF)
    attended = jnp.einsum(
        "kgts,skd->tkgd", attn_probs, value_split, preferred_element_type=F32
    ).astype(BF)
    return attended.reshape(tokens, -1)


def shards(
    residual_in,
    queries,
    key_heads,
    value_heads,
    out_proj,
    norm_gain,
    expert_ids,
    route_weights,
    changed,
    cached_moe,
    gate_proj,
    up_proj,
    down_proj,
):
    plane = lax.axis_size("x") * lax.axis_size("y")
    depth = lax.axis_size("z")
    group_index = lax.axis_index("z")
    tokens = queries.shape[0]

    own_kv = gather_by_exchange(
        jnp.concatenate([key_heads, value_heads], axis=1), ("x", "y"), plane
    )
    all_kv = jnp.concatenate([own_kv, swap_cores(own_kv)], axis=0)
    all_kv = all_kv.reshape(-1, all_kv.shape[-1])

    gate_other, up_other, down_other = (
        swap_cores(gate_proj[0]),
        swap_cores(up_proj[0]),
        swap_cores(down_proj[0]),
    )

    attended = attention(queries, all_kv, key_heads.shape[1] // HD)
    partial_attn = jnp.dot(attended, out_proj, preferred_element_type=F32).astype(BF)
    attn_share = sum_slices(partial_attn, depth)
    mixed_local = (residual_in.astype(F32) + attn_share).astype(BF)

    mixed_full = gather_by_exchange(mixed_local, "z", depth)
    mixed_full = mixed_full.transpose(1, 0, 2).reshape(tokens, -1)
    mixed_float = mixed_full.astype(F32)
    mean_square = jnp.mean(mixed_float * mixed_float, axis=-1, keepdims=True)
    normed = (mixed_float * lax.rsqrt(mean_square + 1e-06) * norm_gain).astype(BF)

    capacity = 2 * tokens * TOP // (EXP_GROUP * depth)
    copies = plane // EXP_GROUP
    local_experts = jnp.arange(EXP_GROUP, dtype=jnp.int32) + group_index * EXP_GROUP
    matches = expert_ids[:, :, None] == local_experts[None, None, :]
    member = jnp.any(matches, axis=1)
    token_weight = jnp.sum(
        jnp.where(matches, route_weights[:, :, None], jnp.zeros((), BF)), axis=1
    )
    rank = jnp.cumsum(member.astype(jnp.int32), axis=0) - 1
    live_rows = member & (changed[:, None] == 1)
    slot_range = jnp.arange(capacity, dtype=jnp.int32)
    select_hit = live_rows.T[:, None, :] & (rank.T[:, None, :] == slot_range[None, :, None])
    selector = select_hit.astype(BF)
    weighted_select = selector * token_weight.T[:, None, :]
    selector = jnp.repeat(selector, copies, axis=0)
    weighted_select = jnp.repeat(weighted_select, copies, axis=0)

    outgoing = jnp.einsum(
        "jct,td->jcd", selector, normed, preferred_element_type=F32
    ).astype(BF)
    outgoing, gate_other, up_other, down_other, weighted_select = lax.optimization_barrier(
        (outgoing, gate_other, up_other, down_other, weighted_select)
    )
    arrived = lax.all_to_all(outgoing, ("x", "y"), split_axis=0, concat_axis=0, tiled=True)
    rows = arrived.reshape(-1, arrived.shape[-1])

    partial_out = expert_partial(
        rows, gate_proj[0], up_proj[0], down_proj[0], gate_other, up_other, down_other
    )
    returned = lax.all_to_all(
        partial_out.reshape(arrived.shape), ("x", "y"), split_axis=0, concat_axis=0, tiled=True
    )
    combined = jnp.einsum(
        "jct,jcd->td", weighted_select, returned, preferred_element_type=F32
    ).astype(BF)
    moe_share = sum_slices(combined, depth)
    moe_value = jnp.where(changed[:, None] == 1, moe_share, cached_moe.astype(F32))
    return (mixed_local.astype(F32) + moe_value).astype(BF)


def solution(mesh):
    cores = 2
    side = int(round((mesh.shape["seq"] // cores) ** 0.5))
    split_mesh = Mesh(
        mesh.devices.reshape(side, side, cores, mesh.shape["exp"]), ("x", "y", "c", "z")
    )
    seq = ("x", "y", "c")
    in_specs = (
        P(seq, "z"),
        P(seq, "z"),
        P(seq, "z"),
        P(seq, "z"),
        P("z", None),
        P(),
        P(seq, None),
        P(seq, None),
        P(seq),
        P(seq, "z"),
        P(("z",) + seq, None, None),
        P(("z",) + seq, None, None),
        P(("z",) + seq, None, None),
    )
    return jax.shard_map(
        shards, mesh=split_mesh, in_specs=in_specs, out_specs=P(seq, "z"), check_vma=False
    )
```

```python
import jax
import jax.numpy as jnp
from jax import lax
from jax.experimental import pallas as pl
from jax.experimental.pallas import tpu as pltpu
from jax.sharding import Mesh, PartitionSpec as P

HD = 128
TOP = 8
EXP_GROUP = 8
BF = jnp.bfloat16
F32 = jnp.float32
PIECES = 4


def swap_cores(array):
    return lax.ppermute(array, "c", [(0, 1), (1, 0)])


def gather_by_exchange(array, axes, count):
    spread = jnp.broadcast_to(array[None], (count,) + array.shape)
    return lax.all_to_all(spread, axes, split_axis=0, concat_axis=0, tiled=True)


def gather_ring(array, depth):
    ahead = [(i, (i + 1) % depth) for i in range(depth)]
    behind = [(i, (i + depth - 1) % depth) for i in range(depth)]
    half = array.shape[0] // 2
    from_behind, from_ahead = [array], [array]
    for step in range(1, depth // 2):
        from_behind.append(lax.ppermute(from_behind[-1], "z", ahead))
        from_ahead.append(lax.ppermute(from_ahead[-1], "z", behind))
    far = jnp.concatenate(
        [
            lax.ppermute(from_behind[-1][:half], "z", ahead),
            lax.ppermute(from_ahead[-1][half:], "z", behind),
        ],
        axis=0,
    )
    pieces = from_ahead + [far] + from_behind[:0:-1]
    twice = jnp.stack(pieces + pieces)
    return lax.dynamic_slice_in_dim(twice, depth - lax.axis_index("z"), depth, 0)


def sum_slices(array, depth):
    tokens, width = array.shape
    slices = array.reshape(tokens, depth, width // depth).transpose(1, 0, 2)
    shares = lax.all_to_all(slices, "z", split_axis=0, concat_axis=0, tiled=True)
    return jnp.sum(shares.astype(F32), axis=0)


def expert_kernel(
    rows, gate_a, up_a, down_a, gate_b, up_b, down_b, out, gate_out, hidden
):
    width = down_a.shape[1] // PIECES
    gates = jnp.concatenate([gate_a[...], gate_b[...]], axis=1)
    gate_out[...] = jnp.dot(rows[...], gates, preferred_element_type=F32)
    ups = jnp.concatenate([up_a[...], up_b[...]], axis=1)
    up_out = jnp.dot(rows[...], ups, preferred_element_type=F32)
    hidden[...] = (jax.nn.silu(gate_out[...]) * up_out).astype(BF)
    for piece in range(PIECES):
        columns = pl.ds(piece * width, width)
        down = jnp.concatenate([down_a[:, columns], down_b[:, columns]], axis=0)
        out[:, columns] = jnp.dot(hidden[...], down, preferred_element_type=F32).astype(BF)


def expert_partial(rows, gate_a, up_a, down_a, gate_b, up_b, down_b):
    count, depth = rows.shape
    part = gate_a.shape[1]
    return pl.pallas_call(
        expert_kernel,
        out_shape=jax.ShapeDtypeStruct((count, depth), BF),
        in_specs=[pl.BlockSpec(memory_space=pltpu.VMEM)] * 7,
        out_specs=pl.BlockSpec(memory_space=pltpu.VMEM),
        scratch_shapes=[
            pltpu.VMEM((count, 2 * part), F32),
            pltpu.VMEM((count, 2 * part), BF),
        ],
        compiler_params=pltpu.CompilerParams(vmem_limit_bytes=16 * 2**20),
        cost_estimate=pl.CostEstimate(
            flops=12 * count * depth * part,
            bytes_accessed=12 * depth * part + 4 * count * depth,
            transcendentals=2 * count * part,
        ),
        name="expert_partial",
    )(*[
        pltpu.with_memory_space_constraint(operand, pltpu.VMEM)
        for operand in (rows, gate_a, up_a, down_a, gate_b, up_b, down_b)
    ])


def attention(queries, all_kv, kv_local):
    tokens = queries.shape[0]
    group_size = queries.shape[1] // HD // kv_local
    width = kv_local * HD
    query_split = queries.reshape(tokens, kv_local, group_size, HD)
    key_split = all_kv[:, :width].reshape(-1, kv_local, HD)
    value_split = all_kv[:, width:].reshape(-1, kv_local, HD)
    scores = jnp.einsum(
        "tkgd,skd->kgts", query_split, key_split, preferred_element_type=F32
    ) * HD ** (-0.5)
    attn_probs = jax.nn.softmax(scores, axis=-1).astype(BF)
    attended = jnp.einsum(
        "kgts,skd->tkgd", attn_probs, value_split, preferred_element_type=F32
    ).astype(BF)
    return attended.reshape(tokens, -1)


def shards(
    residual_in,
    queries,
    key_heads,
    value_heads,
    out_proj,
    norm_gain,
    expert_ids,
    route_weights,
    changed,
    cached_moe,
    gate_proj,
    up_proj,
    down_proj,
):
    plane = lax.axis_size("x") * lax.axis_size("y")
    depth = lax.axis_size("z")
    group_index = lax.axis_index("z")
    tokens = queries.shape[0]

    own_kv = gather_by_exchange(
        jnp.concatenate([key_heads, value_heads], axis=1), ("x", "y"), plane
    )
    all_kv = jnp.concatenate([own_kv, swap_cores(own_kv)], axis=0)
    all_kv = all_kv.reshape(-1, all_kv.shape[-1])

    gate_other, up_other, down_other = (
        swap_cores(gate_proj[0]),
        swap_cores(up_proj[0]),
        swap_cores(down_proj[0]),
    )

    attended = attention(queries, all_kv, key_heads.shape[1] // HD)
    partial_attn = jnp.dot(attended, out_proj, preferred_element_type=F32).astype(BF)
    attn_share = sum_slices(partial_attn, depth)
    mixed_local = (residual_in.astype(F32) + attn_share).astype(BF)

    mixed_full = gather_ring(mixed_local, depth)
    mixed_full = mixed_full.transpose(1, 0, 2).reshape(tokens, -1)
    mixed_float = mixed_full.astype(F32)
    mean_square = jnp.mean(mixed_float * mixed_float, axis=-1, keepdims=True)
    normed = (mixed_float * lax.rsqrt(mean_square + 1e-06) * norm_gain).astype(BF)

    capacity = 2 * tokens * TOP // (EXP_GROUP * depth)
    copies = plane // EXP_GROUP
    local_experts = jnp.arange(EXP_GROUP, dtype=jnp.int32) + group_index * EXP_GROUP
    matches = expert_ids[:, :, None] == local_experts[None, None, :]
    member = jnp.any(matches, axis=1)
    token_weight = jnp.sum(
        jnp.where(matches, route_weights[:, :, None], jnp.zeros((), BF)), axis=1
    )
    rank = jnp.cumsum(member.astype(jnp.int32), axis=0) - 1
    live_rows = member & (changed[:, None] == 1)
    slot_range = jnp.arange(capacity, dtype=jnp.int32)
    select_hit = live_rows.T[:, None, :] & (rank.T[:, None, :] == slot_range[None, :, None])
    selector = select_hit.astype(BF)
    weighted_select = selector * token_weight.T[:, None, :]
    selector = jnp.repeat(selector, copies, axis=0)
    weighted_select = jnp.repeat(weighted_select, copies, axis=0)

    outgoing = jnp.einsum(
        "jct,td->jcd", selector, normed, preferred_element_type=F32
    ).astype(BF)
    outgoing, gate_other, up_other, down_other, weighted_select = lax.optimization_barrier(
        (outgoing, gate_other, up_other, down_other, weighted_select)
    )
    arrived = lax.all_to_all(outgoing, ("x", "y"), split_axis=0, concat_axis=0, tiled=True)
    rows = arrived.reshape(-1, arrived.shape[-1])

    partial_out = expert_partial(
        rows, gate_proj[0], up_proj[0], down_proj[0], gate_other, up_other, down_other
    )
    returned = lax.all_to_all(
        partial_out.reshape(arrived.shape), ("x", "y"), split_axis=0, concat_axis=0, tiled=True
    )
    combined = jnp.einsum(
        "jct,jcd->td", weighted_select, returned, preferred_element_type=F32
    ).astype(BF)
    moe_share = sum_slices(combined, depth)
    moe_value = jnp.where(changed[:, None] == 1, moe_share, cached_moe.astype(F32))
    return (mixed_local.astype(F32) + moe_value).astype(BF)


def solution(mesh):
    cores = 2
    side = int(round((mesh.shape["seq"] // cores) ** 0.5))
    split_mesh = Mesh(
        mesh.devices.reshape(side, side, cores, mesh.shape["exp"]), ("x", "y", "c", "z")
    )
    seq = ("x", "y", "c")
    in_specs = (
        P(seq, "z"),
        P(seq, "z"),
        P(seq, "z"),
        P(seq, "z"),
        P("z", None),
        P(),
        P(seq, None),
        P(seq, None),
        P(seq),
        P(seq, "z"),
        P(("z",) + seq, None, None),
        P(("z",) + seq, None, None),
        P(("z",) + seq, None, None),
    )
    return jax.shard_map(
        shards, mesh=split_mesh, in_specs=in_specs, out_specs=P(seq, "z"), check_vma=False
    )
```

```python
import jax
import jax.numpy as jnp
from jax import lax
from jax.experimental import pallas as pl
from jax.experimental.pallas import tpu as pltpu
from jax.sharding import Mesh, PartitionSpec as P

HD = 128
TOP = 8
EXP_GROUP = 8
BF = jnp.bfloat16
F32 = jnp.float32
PIECES = 4
AHEAD = 2
EIGHTHS = (0, 2, 4, 6, 8)


def swap_cores(array):
    return lax.ppermute(array, "c", [(0, 1), (1, 0)])


def gather_by_exchange(array, axes, count):
    spread = jnp.broadcast_to(array[None], (count,) + array.shape)
    return lax.all_to_all(spread, axes, split_axis=0, concat_axis=0, tiled=True)


def gather_ring(array, depth):
    ahead = [(i, (i + 1) % depth) for i in range(depth)]
    behind = [(i, (i + depth - 1) % depth) for i in range(depth)]
    half = array.shape[0] // 2
    from_behind, from_ahead = [array], [array]
    for step in range(1, depth // 2):
        from_behind.append(lax.ppermute(from_behind[-1], "z", ahead))
        from_ahead.append(lax.ppermute(from_ahead[-1], "z", behind))
    far = jnp.concatenate(
        [
            lax.ppermute(from_behind[-1][:half], "z", ahead),
            lax.ppermute(from_ahead[-1][half:], "z", behind),
        ],
        axis=0,
    )
    pieces = from_ahead + [far] + from_behind[:0:-1]
    twice = jnp.stack(pieces + pieces)
    return lax.dynamic_slice_in_dim(twice, depth - lax.axis_index("z"), depth, 0)


def sum_ring(array, depth):
    tokens, width = array.shape
    width //= depth
    half = tokens // 2
    here = lax.axis_index("z")
    ahead = [(i, (i + 1) % depth) for i in range(depth)]
    behind = [(i, (i + depth - 1) % depth) for i in range(depth)]

    def own(offset):
        start = lax.rem(here + offset, depth) * width
        return lax.dynamic_slice_in_dim(array, start, width, 1)

    def add(mine, arrived):
        return (mine.astype(F32) + arrived.astype(F32)).astype(BF)

    far = own(depth // 2)
    forward = lax.ppermute(far[:half], "z", ahead)
    backward = lax.ppermute(far[half:], "z", behind)
    for offset in range(depth // 2 - 1, 0, -1):
        mine, other = own(offset), own(depth - offset)
        if offset == depth // 2 - 1:
            forward = jnp.concatenate([add(mine[:half], forward), mine[half:]], axis=0)
            backward = jnp.concatenate([other[:half], add(other[half:], backward)], axis=0)
        else:
            forward, backward = add(mine, forward), add(other, backward)
        forward = lax.ppermute(forward, "z", ahead)
        backward = lax.ppermute(backward, "z", behind)
    return own(0).astype(F32) + forward.astype(F32) + backward.astype(F32)


def expert_kernel(
    rows, gate_a, up_a, down_a, gate_b, up_b, down_b, out,
    gates, ups, downs, totals, hidden, in_sem, down_sem,
):
    part = gate_a.shape[1]
    depth = gate_a.shape[0]
    width = depth // PIECES
    bounds = [depth * eighth // 8 for eighth in EIGHTHS]
    steps = len(bounds) - 1

    def in_copies(step):
        here = pl.ds(bounds[step], bounds[step + 1] - bounds[step])
        return [
            pltpu.make_async_copy(part_ref.at[here], store.at[which, here], in_sem.at[2 * which + kind, step])
            for which, pair in enumerate(((gate_a, up_a), (gate_b, up_b)))
            for kind, (part_ref, store) in enumerate(zip(pair, (gates, ups)))
        ]

    def down_copies():
        return [
            pltpu.make_async_copy(down, downs.at[pl.ds(which * part, part)], down_sem.at[which])
            for which, down in enumerate((down_a, down_b))
        ]

    def start(step):
        copies = in_copies(step) if step < steps else down_copies() if step == steps else []
        for copy in copies:
            copy.start()

    for step in range(AHEAD):
        start(step)
    for step in range(steps):
        start(step + AHEAD)
        for copy in in_copies(step):
            copy.wait()
        here = pl.ds(bounds[step], bounds[step + 1] - bounds[step])
        weights = jnp.concatenate(
            [gates[0, here], gates[1, here], ups[0, here], ups[1, here]], axis=1
        )
        product = jnp.dot(rows[:, here], weights, preferred_element_type=F32)
        if step:
            product += totals[...]
        if step < steps - 1:
            totals[...] = product
    gate_out, up_out = product[:, : 2 * part], product[:, 2 * part :]
    hidden[...] = (jax.nn.silu(gate_out) * up_out).astype(BF)
    for copy in down_copies():
        copy.wait()
    for piece in range(PIECES):
        columns = pl.ds(piece * width, width)
        out[:, columns] = jnp.dot(
            hidden[...], downs[:, columns], preferred_element_type=F32
        ).astype(BF)


def expert_partial(rows, *parts):
    count, depth = rows.shape
    part = parts[0].shape[1]
    return pl.pallas_call(
        expert_kernel,
        out_shape=jax.ShapeDtypeStruct((count, depth), BF),
        in_specs=[pl.BlockSpec(memory_space=pltpu.VMEM)]
        + [pl.BlockSpec(memory_space=pl.ANY)] * len(parts),
        out_specs=pl.BlockSpec(memory_space=pltpu.VMEM),
        scratch_shapes=[
            pltpu.VMEM((2, depth, part), BF),
            pltpu.VMEM((2, depth, part), BF),
            pltpu.VMEM((2 * part, depth), BF),
            pltpu.VMEM((count, 4 * part), F32),
            pltpu.VMEM((count, 2 * part), BF),
            pltpu.SemaphoreType.DMA((4, len(EIGHTHS) - 1)),
            pltpu.SemaphoreType.DMA((2,)),
        ],
        compiler_params=pltpu.CompilerParams(vmem_limit_bytes=40 * 2**20),
        cost_estimate=pl.CostEstimate(
            flops=12 * count * depth * part,
            bytes_accessed=12 * depth * part + 4 * count * depth,
            transcendentals=2 * count * part,
        ),
        name="expert_partial",
    )(pltpu.with_memory_space_constraint(rows, pltpu.VMEM), *parts)


def attention(queries, all_kv, kv_local):
    tokens = queries.shape[0]
    group_size = queries.shape[1] // HD // kv_local
    width = kv_local * HD
    query_split = queries.reshape(tokens, kv_local, group_size, HD)
    key_split = all_kv[:, :width].reshape(-1, kv_local, HD)
    value_split = all_kv[:, width:].reshape(-1, kv_local, HD)
    scores = jnp.einsum(
        "tkgd,skd->kgts", query_split, key_split, preferred_element_type=F32
    ) * HD ** (-0.5)
    attn_probs = jax.nn.softmax(scores, axis=-1).astype(BF)
    attended = jnp.einsum(
        "kgts,skd->tkgd", attn_probs, value_split, preferred_element_type=F32
    ).astype(BF)
    return attended.reshape(tokens, -1)


def shards(
    residual_in,
    queries,
    key_heads,
    value_heads,
    out_proj,
    norm_gain,
    expert_ids,
    route_weights,
    changed,
    cached_moe,
    gate_proj,
    up_proj,
    down_proj,
):
    plane = lax.axis_size("x") * lax.axis_size("y")
    depth = lax.axis_size("z")
    group_index = lax.axis_index("z")
    tokens = queries.shape[0]

    own_kv = gather_by_exchange(
        jnp.concatenate([key_heads, value_heads], axis=1), ("x", "y"), plane
    )
    all_kv = jnp.concatenate([own_kv, swap_cores(own_kv)], axis=0)
    all_kv = all_kv.reshape(-1, all_kv.shape[-1])

    other_parts = tuple(swap_cores(part[0]) for part in (gate_proj, up_proj, down_proj))

    attended = attention(queries, all_kv, key_heads.shape[1] // HD)
    partial_attn = jnp.dot(attended, out_proj, preferred_element_type=F32).astype(BF)
    attn_share = sum_ring(partial_attn, depth)
    mixed_local = (residual_in.astype(F32) + attn_share).astype(BF)

    mixed_full = gather_ring(mixed_local, depth)
    mixed_full = mixed_full.transpose(1, 0, 2).reshape(tokens, -1)
    mixed_float = mixed_full.astype(F32)
    mean_square = jnp.mean(mixed_float * mixed_float, axis=-1, keepdims=True)
    normed = (mixed_float * lax.rsqrt(mean_square + 1e-06) * norm_gain).astype(BF)

    capacity = 2 * tokens * TOP // (EXP_GROUP * depth)
    copies = plane // EXP_GROUP
    local_experts = jnp.arange(EXP_GROUP, dtype=jnp.int32) + group_index * EXP_GROUP
    matches = expert_ids[:, :, None] == local_experts[None, None, :]
    member = jnp.any(matches, axis=1)
    token_weight = jnp.sum(
        jnp.where(matches, route_weights[:, :, None], jnp.zeros((), BF)), axis=1
    )
    rank = jnp.cumsum(member.astype(jnp.int32), axis=0) - 1
    live_rows = member & (changed[:, None] == 1)
    slot_range = jnp.arange(capacity, dtype=jnp.int32)
    select_hit = live_rows.T[:, None, :] & (rank.T[:, None, :] == slot_range[None, :, None])
    selector = select_hit.astype(BF)
    weighted_select = selector * token_weight.T[:, None, :]
    selector = jnp.repeat(selector, copies, axis=0)
    weighted_select = jnp.repeat(weighted_select, copies, axis=0)

    outgoing = jnp.einsum(
        "jct,td->jcd", selector, normed, preferred_element_type=F32
    ).astype(BF)
    own_parts = (gate_proj[0], up_proj[0], down_proj[0])
    outgoing, own_parts, other_parts, weighted_select = lax.optimization_barrier(
        (outgoing, own_parts, other_parts, weighted_select)
    )
    arrived = lax.all_to_all(outgoing, ("x", "y"), split_axis=0, concat_axis=0, tiled=True)
    rows = arrived.reshape(-1, arrived.shape[-1])

    partial_out = expert_partial(rows, *own_parts, *other_parts)
    returned = lax.all_to_all(
        partial_out.reshape(arrived.shape), ("x", "y"), split_axis=0, concat_axis=0, tiled=True
    )
    combined = jnp.einsum(
        "jct,jcd->td", weighted_select, returned, preferred_element_type=F32
    ).astype(BF)
    moe_share = sum_ring(combined, depth)
    moe_value = jnp.where(changed[:, None] == 1, moe_share, cached_moe.astype(F32))
    return (mixed_local.astype(F32) + moe_value).astype(BF)


def solution(mesh):
    cores = 2
    side = int(round((mesh.shape["seq"] // cores) ** 0.5))
    split_mesh = Mesh(
        mesh.devices.reshape(side, side, cores, mesh.shape["exp"]), ("x", "y", "c", "z")
    )
    seq = ("x", "y", "c")
    in_specs = (
        P(seq, "z"),
        P(seq, "z"),
        P(seq, "z"),
        P(seq, "z"),
        P("z", None),
        P(),
        P(seq, None),
        P(seq, None),
        P(seq),
        P(seq, "z"),
        P(("z",) + seq, None, None),
        P(("z",) + seq, None, None),
        P(("z",) + seq, None, None),
    )
    return jax.shard_map(
        shards, mesh=split_mesh, in_specs=in_specs, out_specs=P(seq, "z"), check_vma=False
    )
```

```python
import jax
import jax.numpy as jnp
from jax import lax
from jax.experimental import pallas as pl
from jax.experimental.pallas import tpu as pltpu
from jax.sharding import Mesh, PartitionSpec as P

HD = 128
TOP = 8
EXP_GROUP = 8
SLICE = 512
BF = jnp.bfloat16
F32 = jnp.float32
PIECES = 4
AHEAD = 2
EIGHTHS = (0, 2, 4, 6, 8)


def swap_cores(array):
    return lax.ppermute(array, "c", [(0, 1), (1, 0)])


def gather_by_exchange(array, axes, count):
    spread = jnp.broadcast_to(array[None], (count,) + array.shape)
    return lax.all_to_all(spread, axes, split_axis=0, concat_axis=0, tiled=True)


def gather_ring(piece, depth):
    ahead = [(i, (i + 1) % depth) for i in range(depth)]
    behind = [(i, (i + depth - 1) % depth) for i in range(depth)]
    half = piece.shape[0] // 2
    from_behind, from_ahead = [piece], [piece]
    for _ in range(1, depth // 2):
        from_behind.append(lax.ppermute(from_behind[-1], "z", ahead))
        from_ahead.append(lax.ppermute(from_ahead[-1], "z", behind))
    far = (
        lax.ppermute(from_behind[-1][:half], "z", ahead),
        lax.ppermute(from_ahead[-1][half:], "z", behind),
    )
    return from_ahead + [far] + from_behind[:0:-1]


def sum_ring(slices, depth):
    ahead = [(i, (i + 1) % depth) for i in range(depth)]
    behind = [(i, (i + depth - 1) % depth) for i in range(depth)]

    def add(mine, arrived):
        return (mine.astype(F32) + arrived.astype(F32)).astype(BF)

    far = depth // 2
    first, second = slices[far]
    half = first.shape[0]
    forward = lax.ppermute(first, "z", ahead)
    backward = lax.ppermute(second, "z", behind)
    for offset in range(far - 1, 0, -1):
        mine, other = slices[offset], slices[depth - offset]
        if offset == far - 1:
            forward = jnp.concatenate([add(mine[:half], forward), mine[half:]], axis=0)
            backward = jnp.concatenate([other[:half], add(other[half:], backward)], axis=0)
        else:
            forward, backward = add(mine, forward), add(other, backward)
        forward = lax.ppermute(forward, "z", ahead)
        backward = lax.ppermute(backward, "z", behind)
    return slices[0].astype(F32) + forward.astype(F32) + backward.astype(F32)


def in_vmem(*operands):
    return [pltpu.with_memory_space_constraint(operand, pltpu.VMEM) for operand in operands]


def slice_shapes(depth, rows, width):
    shapes = [jax.ShapeDtypeStruct((rows, width), BF)] * (depth + 1)
    shapes[depth // 2] = shapes[depth // 2 + 1] = jax.ShapeDtypeStruct((rows // 2, width), BF)
    return shapes


def pair_far(slices):
    far = (len(slices) - 1) // 2
    return slices[:far] + [(slices[far], slices[far + 1])] + slices[far + 2 :]


def store_slices(group, outs, product_of):
    depth = len(outs) - 1
    far = depth // 2
    half, width = outs[far].shape
    for offset in range(depth):
        start = pl.multiple_of(lax.rem(group + offset, depth) * width, width)
        product = product_of(pl.ds(start, width)).astype(BF)
        if offset < far:
            outs[offset][...] = product
        elif offset > far:
            outs[offset + 1][...] = product
        else:
            outs[far][...] = product[:half]
            outs[far + 1][...] = product[half:]


def attention_kernel(group, queries, own_kv, other_kv, out_proj, out):
    tokens, width = queries.shape
    heads = width // HD
    stacked = jnp.concatenate(
        [queries[:, head * HD : (head + 1) * HD] for head in range(heads)], axis=0
    )
    contract = (((1,), (1,)), ((), ()))
    scores = [
        lax.dot_general(stacked, kv[:, :HD], contract, preferred_element_type=F32)
        for kv in (own_kv, other_kv)
    ]
    top = jnp.maximum(*[jnp.max(part, axis=1, keepdims=True) for part in scores])
    weights = [jnp.exp((part - top) * HD ** (-0.5)) for part in scores]
    total = sum(jnp.sum(part, axis=1, keepdims=True) for part in weights)
    values = sum(
        jnp.dot(part.astype(BF), kv[:, HD:], preferred_element_type=F32)
        for part, kv in zip(weights, (own_kv, other_kv))
    )
    attended = (values / total).astype(BF)
    attended = jnp.concatenate(
        [attended[head * tokens : (head + 1) * tokens] for head in range(heads)], axis=1
    )
    depth = out_proj.shape[1] // SLICE
    for offset in range(depth):
        start = pl.multiple_of(lax.rem(group[0] + offset, depth) * SLICE, SLICE)
        product = jnp.dot(
            attended, out_proj[:, pl.ds(start, SLICE)], preferred_element_type=F32
        )
        out[:, offset * SLICE : (offset + 1) * SLICE] = product.astype(BF)


def attention_slices(group, queries, own_kv, other_kv, out_proj, depth):
    tokens, width = queries.shape
    total = pl.pallas_call(
        attention_kernel,
        out_shape=jax.ShapeDtypeStruct((tokens, out_proj.shape[1]), BF),
        in_specs=[pl.BlockSpec(memory_space=pltpu.SMEM)]
        + [pl.BlockSpec(memory_space=pltpu.VMEM)] * 4,
        out_specs=pl.BlockSpec(memory_space=pltpu.VMEM),
        compiler_params=pltpu.CompilerParams(vmem_limit_bytes=32 * 2**20),
        name="attention",
    )(group, *in_vmem(queries, own_kv, other_kv, out_proj))
    slices = [total[:, offset * SLICE : (offset + 1) * SLICE] for offset in range(depth)]
    far = slices[depth // 2]
    slices[depth // 2] = (far[: tokens // 2], far[tokens // 2 :])
    return slices


def dispatch_kernel(group, selector, gain, *refs):
    *pieces, out = refs
    far = (len(pieces) - 1) // 2
    whole = [piece[...].astype(F32) for piece in pieces]
    whole[far : far + 2] = [jnp.concatenate(whole[far : far + 2], axis=0)]
    depth = len(whole)
    width = whole[0].shape[1]
    square = sum(jnp.sum(piece * piece, axis=1, keepdims=True) for piece in whole)
    scale = lax.rsqrt(square / (depth * width) + 1e-06)
    for offset, piece in enumerate(whole):
        start = pl.multiple_of(lax.rem(group[0] + offset, depth) * width, width)
        columns = pl.ds(start, width)
        normed = (piece * scale * gain[:, columns]).astype(BF)
        rows = jnp.dot(selector[...], normed, preferred_element_type=F32).astype(BF)
        rows = rows.reshape(out.shape[0], out.shape[2], width)
        for copy in range(out.shape[1]):
            out[:, copy, :, columns] = rows


def dispatch_rows(group, selector, gain, pieces, experts, copies):
    far = len(pieces) // 2
    flat = pieces[:far] + list(pieces[far]) + pieces[far + 1 :]
    width = gain.shape[1]
    return pl.pallas_call(
        dispatch_kernel,
        out_shape=jax.ShapeDtypeStruct(
            (experts, copies, selector.shape[0] // experts, width), BF
        ),
        in_specs=[pl.BlockSpec(memory_space=pltpu.SMEM)]
        + [pl.BlockSpec(memory_space=pltpu.VMEM)] * (2 + len(flat)),
        out_specs=pl.BlockSpec(memory_space=pltpu.VMEM),
        compiler_params=pltpu.CompilerParams(vmem_limit_bytes=24 * 2**20),
        name="dispatch",
    )(group, *in_vmem(selector, gain, *flat))


def combine_kernel(group, weights, returned, *outs):
    store_slices(
        group[0],
        outs,
        lambda columns: jnp.dot(
            weights[...], returned[:, columns], preferred_element_type=F32
        ),
    )


def combine_slices(group, weights, returned, depth):
    shapes = slice_shapes(depth, weights.shape[0], returned.shape[1] // depth)
    slices = pl.pallas_call(
        combine_kernel,
        out_shape=shapes,
        in_specs=[pl.BlockSpec(memory_space=pltpu.SMEM)]
        + [pl.BlockSpec(memory_space=pltpu.VMEM)] * 2,
        out_specs=[pl.BlockSpec(memory_space=pltpu.VMEM)] * len(shapes),
        compiler_params=pltpu.CompilerParams(vmem_limit_bytes=16 * 2**20),
        name="combine",
    )(group, *in_vmem(weights, returned))
    return pair_far(list(slices))


def expert_kernel(
    rows, gate_a, up_a, down_a, gate_b, up_b, down_b, out,
    gates, ups, downs, totals, hidden, in_sem, down_sem,
):
    part = gate_a.shape[1]
    depth = gate_a.shape[0]
    width = depth // PIECES
    bounds = [depth * eighth // 8 for eighth in EIGHTHS]
    steps = len(bounds) - 1

    def in_copies(step):
        here = pl.ds(bounds[step], bounds[step + 1] - bounds[step])
        return [
            pltpu.make_async_copy(part_ref.at[here], store.at[which, here], in_sem.at[2 * which + kind, step])
            for which, pair in enumerate(((gate_a, up_a), (gate_b, up_b)))
            for kind, (part_ref, store) in enumerate(zip(pair, (gates, ups)))
        ]

    def down_copies():
        return [
            pltpu.make_async_copy(down, downs.at[pl.ds(which * part, part)], down_sem.at[which])
            for which, down in enumerate((down_a, down_b))
        ]

    def start(step):
        copies = in_copies(step) if step < steps else down_copies() if step == steps else []
        for copy in copies:
            copy.start()

    for step in range(AHEAD):
        start(step)
    for step in range(steps):
        start(step + AHEAD)
        for copy in in_copies(step):
            copy.wait()
        here = pl.ds(bounds[step], bounds[step + 1] - bounds[step])
        weights = jnp.concatenate(
            [gates[0, here], gates[1, here], ups[0, here], ups[1, here]], axis=1
        )
        product = jnp.dot(rows[:, here], weights, preferred_element_type=F32)
        if step:
            product += totals[...]
        if step < steps - 1:
            totals[...] = product
    gate_out, up_out = product[:, : 2 * part], product[:, 2 * part :]
    hidden[...] = (jax.nn.silu(gate_out) * up_out).astype(BF)
    for copy in down_copies():
        copy.wait()
    for piece in range(PIECES):
        columns = pl.ds(piece * width, width)
        out[:, columns] = jnp.dot(
            hidden[...], downs[:, columns], preferred_element_type=F32
        ).astype(BF)


def expert_partial(rows, *parts):
    count, depth = rows.shape
    part = parts[0].shape[1]
    return pl.pallas_call(
        expert_kernel,
        out_shape=jax.ShapeDtypeStruct((count, depth), BF),
        in_specs=[pl.BlockSpec(memory_space=pltpu.VMEM)]
        + [pl.BlockSpec(memory_space=pl.ANY)] * len(parts),
        out_specs=pl.BlockSpec(memory_space=pltpu.VMEM),
        scratch_shapes=[
            pltpu.VMEM((2, depth, part), BF),
            pltpu.VMEM((2, depth, part), BF),
            pltpu.VMEM((2 * part, depth), BF),
            pltpu.VMEM((count, 4 * part), F32),
            pltpu.VMEM((count, 2 * part), BF),
            pltpu.SemaphoreType.DMA((4, len(EIGHTHS) - 1)),
            pltpu.SemaphoreType.DMA((2,)),
        ],
        compiler_params=pltpu.CompilerParams(vmem_limit_bytes=40 * 2**20),
        cost_estimate=pl.CostEstimate(
            flops=12 * count * depth * part,
            bytes_accessed=12 * depth * part + 4 * count * depth,
            transcendentals=2 * count * part,
        ),
        name="expert_partial",
    )(pltpu.with_memory_space_constraint(rows, pltpu.VMEM), *parts)


def shards(
    residual_in,
    queries,
    key_heads,
    value_heads,
    out_proj,
    norm_gain,
    expert_ids,
    route_weights,
    changed,
    cached_moe,
    gate_proj,
    up_proj,
    down_proj,
):
    plane = lax.axis_size("x") * lax.axis_size("y")
    depth = lax.axis_size("z")
    group_index = lax.axis_index("z")
    tokens = queries.shape[0]

    own_kv = gather_by_exchange(
        jnp.concatenate([key_heads, value_heads], axis=1), ("x", "y"), plane
    )
    own_kv = own_kv.reshape(-1, own_kv.shape[-1])
    other_kv = swap_cores(own_kv)

    other_parts = tuple(swap_cores(part[0]) for part in (gate_proj, up_proj, down_proj))

    group = group_index.astype(jnp.int32).reshape(1)
    attn_share = sum_ring(
        attention_slices(group, queries, own_kv, other_kv, out_proj, depth), depth
    )
    mixed_local = (residual_in.astype(F32) + attn_share).astype(BF)
    mixed_pieces = gather_ring(mixed_local, depth)

    capacity = 2 * tokens * TOP // (EXP_GROUP * depth)
    copies = plane // EXP_GROUP
    local_experts = jnp.arange(EXP_GROUP, dtype=jnp.int32) + group_index * EXP_GROUP
    matches = expert_ids[:, :, None] == local_experts[None, None, :]
    member = jnp.any(matches, axis=1)
    token_weight = jnp.sum(
        jnp.where(matches, route_weights[:, :, None], jnp.zeros((), BF)), axis=1
    )
    rank = jnp.cumsum(member.astype(jnp.int32), axis=0) - 1
    live_rows = member & (changed[:, None] == 1)
    slot_range = jnp.arange(capacity, dtype=jnp.int32)
    select_hit = live_rows.T[:, None, :] & (rank.T[:, None, :] == slot_range[None, :, None])
    selector = select_hit.astype(BF)
    weighted_select = selector * token_weight.T[:, None, :]
    weighted_select = jnp.repeat(weighted_select, copies, axis=0)
    weighted_select = weighted_select.reshape(-1, tokens).T
    outgoing = dispatch_rows(
        group,
        selector.reshape(-1, tokens),
        norm_gain.reshape(1, -1),
        mixed_pieces,
        EXP_GROUP,
        copies,
    )
    outgoing = outgoing.reshape(plane, capacity, -1)
    own_parts = (gate_proj[0], up_proj[0], down_proj[0])
    outgoing, own_parts, other_parts, weighted_select = lax.optimization_barrier(
        (outgoing, own_parts, other_parts, weighted_select)
    )
    arrived = lax.all_to_all(outgoing, ("x", "y"), split_axis=0, concat_axis=0, tiled=True)
    rows = arrived.reshape(-1, arrived.shape[-1])

    partial_out = expert_partial(rows, *own_parts, *other_parts)
    returned = lax.all_to_all(
        partial_out.reshape(arrived.shape), ("x", "y"), split_axis=0, concat_axis=0, tiled=True
    )
    moe_share = sum_ring(
        combine_slices(group, weighted_select, returned.reshape(rows.shape), depth), depth
    )
    moe_value = jnp.where(changed[:, None] == 1, moe_share, cached_moe.astype(F32))
    return (mixed_local.astype(F32) + moe_value).astype(BF)


def solution(mesh):
    cores = 2
    side = int(round((mesh.shape["seq"] // cores) ** 0.5))
    split_mesh = Mesh(
        mesh.devices.reshape(side, side, cores, mesh.shape["exp"]), ("x", "y", "c", "z")
    )
    seq = ("x", "y", "c")
    in_specs = (
        P(seq, "z"),
        P(seq, "z"),
        P(seq, "z"),
        P(seq, "z"),
        P("z", None),
        P(),
        P(seq, None),
        P(seq, None),
        P(seq),
        P(seq, "z"),
        P(("z",) + seq, None, None),
        P(("z",) + seq, None, None),
        P(("z",) + seq, None, None),
    )
    return jax.shard_map(
        shards, mesh=split_mesh, in_specs=in_specs, out_specs=P(seq, "z"), check_vma=False
    )
```

```python
import jax
import jax.numpy as jnp
from jax import lax
from jax.experimental import pallas as pl
from jax.experimental.pallas import tpu as pltpu
from jax.sharding import Mesh, PartitionSpec as P

HD = 128
TOP = 8
EXP_GROUP = 8
SLICE = 512
BF = jnp.bfloat16
F32 = jnp.float32
PIECES = 4
AHEAD = 2
EIGHTHS = (0, 2, 4, 6, 8)


def swap_cores(array):
    return lax.ppermute(array, "c", [(0, 1), (1, 0)])


def gather_by_exchange(array, axes, count):
    spread = jnp.broadcast_to(array[None], (count,) + array.shape)
    return lax.all_to_all(spread, axes, split_axis=0, concat_axis=0, tiled=True)


def shift(array, hops):
    depth = lax.axis_size("z")
    return lax.ppermute(array, "z", [(i, (i + hops) % depth) for i in range(depth)])


def gather_ring(piece, depth):
    ahead = [(i, (i + 1) % depth) for i in range(depth)]
    behind = [(i, (i + depth - 1) % depth) for i in range(depth)]
    half = piece.shape[0] // 2
    from_behind, from_ahead = [piece], [piece]
    for _ in range(1, depth // 2):
        from_behind.append(lax.ppermute(from_behind[-1], "z", ahead))
        from_ahead.append(lax.ppermute(from_ahead[-1], "z", behind))
    far = (
        lax.ppermute(from_behind[-1][:half], "z", ahead),
        lax.ppermute(from_ahead[-1][half:], "z", behind),
    )
    return from_ahead + [far] + from_behind[:0:-1]


def sum_ring(slices, depth):
    assert depth == 8
    first, second = slices[4]
    half = first.shape[0]
    near = shift(slices[3], 1).astype(F32), shift(slices[5], -1).astype(F32)
    far = shift(first, 2).astype(F32), shift(second, -2).astype(F32)
    forward = slices[2].astype(F32) + near[0]
    backward = slices[6].astype(F32) + near[1]
    forward = jnp.concatenate([forward[:half] + far[0], forward[half:]], axis=0)
    backward = jnp.concatenate([backward[:half], backward[half:] + far[1]], axis=0)
    arrived = [
        shift(slices[1], 1),
        shift(slices[7], -1),
        shift(forward.astype(BF), 2),
        shift(backward.astype(BF), -2),
    ]
    return sum((part.astype(F32) for part in arrived), slices[0].astype(F32))


def sum_long_ring(slices, depth):
    ahead = [(i, (i + 1) % depth) for i in range(depth)]
    behind = [(i, (i + depth - 1) % depth) for i in range(depth)]

    def add(mine, arrived):
        return (mine.astype(F32) + arrived.astype(F32)).astype(BF)

    far = depth // 2
    first, second = slices[far]
    half = first.shape[0]
    forward = lax.ppermute(first, "z", ahead)
    backward = lax.ppermute(second, "z", behind)
    for offset in range(far - 1, 0, -1):
        mine, other = slices[offset], slices[depth - offset]
        if offset == far - 1:
            forward = jnp.concatenate([add(mine[:half], forward), mine[half:]], axis=0)
            backward = jnp.concatenate([other[:half], add(other[half:], backward)], axis=0)
        else:
            forward, backward = add(mine, forward), add(other, backward)
        forward = lax.ppermute(forward, "z", ahead)
        backward = lax.ppermute(backward, "z", behind)
    return slices[0].astype(F32) + forward.astype(F32) + backward.astype(F32)


def in_vmem(*operands):
    return [pltpu.with_memory_space_constraint(operand, pltpu.VMEM) for operand in operands]


def in_hbm(operand):
    return pltpu.with_memory_space_constraint(operand, pltpu.HBM)


def slice_shapes(depth, rows, width):
    shapes = [jax.ShapeDtypeStruct((rows, width), BF)] * (depth + 1)
    shapes[depth // 2] = shapes[depth // 2 + 1] = jax.ShapeDtypeStruct((rows // 2, width), BF)
    return shapes


def pair_far(slices):
    far = (len(slices) - 1) // 2
    return slices[:far] + [(slices[far], slices[far + 1])] + slices[far + 2 :]


def store_slices(group, outs, product_of):
    depth = len(outs) - 1
    far = depth // 2
    half, width = outs[far].shape
    for offset in range(depth):
        start = pl.multiple_of(lax.rem(group + offset, depth) * width, width)
        product = product_of(pl.ds(start, width)).astype(BF)
        if offset < far:
            outs[offset][...] = product
        elif offset > far:
            outs[offset + 1][...] = product
        else:
            outs[far][...] = product[:half]
            outs[far + 1][...] = product[half:]


def attention_kernel(
    group, queries, own_kv, other_kv, out_proj_hbm, out, out_proj, proj_sem
):
    proj_copy = pltpu.make_async_copy(out_proj_hbm, out_proj, proj_sem)
    proj_copy.start()
    tokens, width = queries.shape
    heads = width // HD
    stacked = jnp.concatenate(
        [queries[:, head * HD : (head + 1) * HD] for head in range(heads)], axis=0
    )
    contract = (((1,), (1,)), ((), ()))
    scores = [
        lax.dot_general(stacked, kv[:, :HD], contract, preferred_element_type=F32)
        for kv in (own_kv, other_kv)
    ]
    top = jnp.maximum(*[jnp.max(part, axis=1, keepdims=True) for part in scores])
    weights = [jnp.exp((part - top) * HD ** (-0.5)) for part in scores]
    total = sum(jnp.sum(part, axis=1, keepdims=True) for part in weights)
    values = sum(
        jnp.dot(part.astype(BF), kv[:, HD:], preferred_element_type=F32)
        for part, kv in zip(weights, (own_kv, other_kv))
    )
    attended = (values / total).astype(BF)
    attended = jnp.concatenate(
        [attended[head * tokens : (head + 1) * tokens] for head in range(heads)], axis=1
    )
    proj_copy.wait()
    depth = out_proj.shape[1] // SLICE
    for offset in range(depth):
        start = pl.multiple_of(lax.rem(group[0] + offset, depth) * SLICE, SLICE)
        product = jnp.dot(
            attended, out_proj[:, pl.ds(start, SLICE)], preferred_element_type=F32
        )
        out[:, offset * SLICE : (offset + 1) * SLICE] = product.astype(BF)


def attention_slices(group, queries, own_kv, other_kv, out_proj, depth):
    tokens, width = queries.shape
    total = pl.pallas_call(
        attention_kernel,
        out_shape=jax.ShapeDtypeStruct((tokens, out_proj.shape[1]), BF),
        in_specs=[pl.BlockSpec(memory_space=pltpu.SMEM)]
        + [pl.BlockSpec(memory_space=pltpu.VMEM)] * 3
        + [pl.BlockSpec(memory_space=pl.ANY)],
        out_specs=pl.BlockSpec(memory_space=pltpu.VMEM),
        scratch_shapes=[pltpu.VMEM(out_proj.shape, BF), pltpu.SemaphoreType.DMA],
        compiler_params=pltpu.CompilerParams(vmem_limit_bytes=32 * 2**20),
        name="attention",
    )(group, *in_vmem(queries, own_kv, other_kv), in_hbm(out_proj))
    slices = [total[:, offset * SLICE : (offset + 1) * SLICE] for offset in range(depth)]
    far = slices[depth // 2]
    slices[depth // 2] = (far[: tokens // 2], far[tokens // 2 :])
    return slices


def dispatch_kernel(group, selector, gain, *refs):
    *pieces, out = refs
    far = (len(pieces) - 1) // 2
    whole = [piece[...].astype(F32) for piece in pieces]
    whole[far : far + 2] = [jnp.concatenate(whole[far : far + 2], axis=0)]
    depth = len(whole)
    width = whole[0].shape[1]
    square = sum(jnp.sum(piece * piece, axis=1, keepdims=True) for piece in whole)
    scale = lax.rsqrt(square / (depth * width) + 1e-06)
    for offset, piece in enumerate(whole):
        start = pl.multiple_of(lax.rem(group[0] + offset, depth) * width, width)
        columns = pl.ds(start, width)
        normed = (piece * scale * gain[:, columns]).astype(BF)
        rows = jnp.dot(selector[...], normed, preferred_element_type=F32).astype(BF)
        rows = rows.reshape(out.shape[0], out.shape[2], width)
        for copy in range(out.shape[1]):
            out[:, copy, :, columns] = rows


def dispatch_rows(group, selector, gain, pieces, experts, copies):
    far = len(pieces) // 2
    flat = pieces[:far] + list(pieces[far]) + pieces[far + 1 :]
    width = gain.shape[1]
    return pl.pallas_call(
        dispatch_kernel,
        out_shape=jax.ShapeDtypeStruct(
            (experts, copies, selector.shape[0] // experts, width), BF
        ),
        in_specs=[pl.BlockSpec(memory_space=pltpu.SMEM)]
        + [pl.BlockSpec(memory_space=pltpu.VMEM)] * (2 + len(flat)),
        out_specs=pl.BlockSpec(memory_space=pltpu.VMEM),
        compiler_params=pltpu.CompilerParams(vmem_limit_bytes=24 * 2**20),
        name="dispatch",
    )(group, *in_vmem(selector, gain, *flat))


def combine_kernel(group, weights, returned, *outs):
    store_slices(
        group[0],
        outs,
        lambda columns: jnp.dot(
            weights[...], returned[:, columns], preferred_element_type=F32
        ),
    )


def combine_slices(group, weights, returned, depth):
    shapes = slice_shapes(depth, weights.shape[0], returned.shape[1] // depth)
    slices = pl.pallas_call(
        combine_kernel,
        out_shape=shapes,
        in_specs=[pl.BlockSpec(memory_space=pltpu.SMEM)]
        + [pl.BlockSpec(memory_space=pltpu.VMEM)] * 2,
        out_specs=[pl.BlockSpec(memory_space=pltpu.VMEM)] * len(shapes),
        compiler_params=pltpu.CompilerParams(vmem_limit_bytes=16 * 2**20),
        name="combine",
    )(group, *in_vmem(weights, returned))
    return pair_far(list(slices))


def expert_kernel(
    rows, gate_a, up_a, down_a, gate_b, up_b, down_b, out,
    gates, ups, downs, totals, hidden, in_sem, down_sem,
):
    part = gate_a.shape[1]
    depth = gate_a.shape[0]
    width = depth // PIECES
    bounds = [depth * eighth // 8 for eighth in EIGHTHS]
    steps = len(bounds) - 1

    def in_copies(step):
        here = pl.ds(bounds[step], bounds[step + 1] - bounds[step])
        return [
            pltpu.make_async_copy(part_ref.at[here], store.at[which, here], in_sem.at[2 * which + kind, step])
            for which, pair in enumerate(((gate_a, up_a), (gate_b, up_b)))
            for kind, (part_ref, store) in enumerate(zip(pair, (gates, ups)))
        ]

    def down_copies():
        return [
            pltpu.make_async_copy(down, downs.at[pl.ds(which * part, part)], down_sem.at[which])
            for which, down in enumerate((down_a, down_b))
        ]

    def start(step):
        copies = in_copies(step) if step < steps else down_copies() if step == steps else []
        for copy in copies:
            copy.start()

    for step in range(AHEAD):
        start(step)
    for step in range(steps):
        start(step + AHEAD)
        for copy in in_copies(step):
            copy.wait()
        here = pl.ds(bounds[step], bounds[step + 1] - bounds[step])
        weights = jnp.concatenate(
            [gates[0, here], gates[1, here], ups[0, here], ups[1, here]], axis=1
        )
        product = jnp.dot(rows[:, here], weights, preferred_element_type=F32)
        if step:
            product += totals[...]
        if step < steps - 1:
            totals[...] = product
    gate_out, up_out = product[:, : 2 * part], product[:, 2 * part :]
    hidden[...] = (jax.nn.silu(gate_out) * up_out).astype(BF)
    for copy in down_copies():
        copy.wait()
    for piece in range(PIECES):
        columns = pl.ds(piece * width, width)
        out[:, columns] = jnp.dot(
            hidden[...], downs[:, columns], preferred_element_type=F32
        ).astype(BF)


def expert_partial(rows, *parts):
    count, depth = rows.shape
    part = parts[0].shape[1]
    return pl.pallas_call(
        expert_kernel,
        out_shape=pltpu.VMEM((count, depth), BF),
        in_specs=[pl.BlockSpec(memory_space=pltpu.VMEM)]
        + [pl.BlockSpec(memory_space=pl.ANY)] * len(parts),
        out_specs=pl.BlockSpec(memory_space=pltpu.VMEM),
        scratch_shapes=[
            pltpu.VMEM((2, depth, part), BF),
            pltpu.VMEM((2, depth, part), BF),
            pltpu.VMEM((2 * part, depth), BF),
            pltpu.VMEM((count, 4 * part), F32),
            pltpu.VMEM((count, 2 * part), BF),
            pltpu.SemaphoreType.DMA((4, len(EIGHTHS) - 1)),
            pltpu.SemaphoreType.DMA((2,)),
        ],
        compiler_params=pltpu.CompilerParams(vmem_limit_bytes=36 * 2**20),
        cost_estimate=pl.CostEstimate(
            flops=12 * count * depth * part,
            bytes_accessed=12 * depth * part + 4 * count * depth,
            transcendentals=2 * count * part,
        ),
        name="expert_partial",
    )(pltpu.with_memory_space_constraint(rows, pltpu.VMEM), *parts)


def shards(
    residual_in,
    queries,
    key_heads,
    value_heads,
    out_proj,
    norm_gain,
    expert_ids,
    route_weights,
    changed,
    cached_moe,
    gate_proj,
    up_proj,
    down_proj,
):
    plane = lax.axis_size("x") * lax.axis_size("y")
    depth = lax.axis_size("z")
    group_index = lax.axis_index("z")
    tokens = queries.shape[0]

    own_kv = gather_by_exchange(
        jnp.concatenate([key_heads, value_heads], axis=1), ("x", "y"), plane
    )
    own_kv = own_kv.reshape(-1, own_kv.shape[-1])
    other_kv = swap_cores(own_kv)

    other_parts = tuple(swap_cores(part[0]) for part in (gate_proj, up_proj, down_proj))

    group = group_index.astype(jnp.int32).reshape(1)
    attn_share = sum_long_ring(
        attention_slices(group, queries, own_kv, other_kv, out_proj, depth), depth
    )
    mixed_local = (residual_in.astype(F32) + attn_share).astype(BF)
    mixed_pieces = gather_ring(mixed_local, depth)

    capacity = 2 * tokens * TOP // (EXP_GROUP * depth)
    copies = plane // EXP_GROUP
    local_experts = jnp.arange(EXP_GROUP, dtype=jnp.int32) + group_index * EXP_GROUP
    matches = expert_ids[:, :, None] == local_experts[None, None, :]
    member = jnp.any(matches, axis=1)
    token_weight = jnp.sum(
        jnp.where(matches, route_weights[:, :, None], jnp.zeros((), BF)), axis=1
    )
    rank = jnp.cumsum(member.astype(jnp.int32), axis=0) - 1
    live_rows = member & (changed[:, None] == 1)
    slot_range = jnp.arange(capacity, dtype=jnp.int32)
    select_hit = live_rows.T[:, None, :] & (rank.T[:, None, :] == slot_range[None, :, None])
    selector = select_hit.astype(BF)
    weighted_select = selector * token_weight.T[:, None, :]
    weighted_select = jnp.repeat(weighted_select, copies, axis=0)
    weighted_select = weighted_select.reshape(-1, tokens).T
    outgoing = dispatch_rows(
        group,
        selector.reshape(-1, tokens),
        norm_gain.reshape(1, -1),
        mixed_pieces,
        EXP_GROUP,
        copies,
    )
    outgoing = outgoing.reshape(plane, capacity, -1)
    own_parts = (gate_proj[0], up_proj[0], down_proj[0])
    outgoing, own_parts, other_parts, weighted_select = lax.optimization_barrier(
        (outgoing, own_parts, other_parts, weighted_select)
    )
    arrived = lax.all_to_all(outgoing, ("x", "y"), split_axis=0, concat_axis=0, tiled=True)
    rows = arrived.reshape(-1, arrived.shape[-1])

    partial_out = expert_partial(rows, *own_parts, *other_parts)
    returned = lax.all_to_all(
        partial_out.reshape(arrived.shape), ("x", "y"), split_axis=0, concat_axis=0, tiled=True
    )
    moe_share = sum_ring(
        combine_slices(group, weighted_select, returned.reshape(rows.shape), depth), depth
    )
    moe_value = jnp.where(changed[:, None] == 1, moe_share, cached_moe.astype(F32))
    return (mixed_local.astype(F32) + moe_value).astype(BF)


def solution(mesh):
    cores = 2
    side = int(round((mesh.shape["seq"] // cores) ** 0.5))
    split_mesh = Mesh(
        mesh.devices.reshape(side, side, cores, mesh.shape["exp"]), ("x", "y", "c", "z")
    )
    seq = ("x", "y", "c")
    in_specs = (
        P(seq, "z"),
        P(seq, "z"),
        P(seq, "z"),
        P(seq, "z"),
        P("z", None),
        P(),
        P(seq, None),
        P(seq, None),
        P(seq),
        P(seq, "z"),
        P(("z",) + seq, None, None),
        P(("z",) + seq, None, None),
        P(("z",) + seq, None, None),
    )
    return jax.shard_map(
        shards, mesh=split_mesh, in_specs=in_specs, out_specs=P(seq, "z"), check_vma=False
    )
```

```python
import jax
import jax.numpy as jnp
from jax import lax
from jax.experimental import pallas as pl
from jax.experimental.pallas import tpu as pltpu
from jax.sharding import Mesh, PartitionSpec as P

HD = 128
TOP = 8
EXP_GROUP = 8
SLICE = 512
BF = jnp.bfloat16
F32 = jnp.float32
PIECES = 4
AHEAD = 2
EIGHTHS = (0, 2, 4, 6, 8)


def swap_cores(array):
    return lax.ppermute(array, "c", [(0, 1), (1, 0)])


def gather_by_exchange(array, axes, count):
    spread = jnp.broadcast_to(array[None], (count,) + array.shape)
    return lax.all_to_all(spread, axes, split_axis=0, concat_axis=0, tiled=True)


def shift(array, hops):
    depth = lax.axis_size("z")
    return lax.ppermute(array, "z", [(i, (i + hops) % depth) for i in range(depth)])


def gather_ring(piece, depth):
    ahead = [(i, (i + 1) % depth) for i in range(depth)]
    behind = [(i, (i + depth - 1) % depth) for i in range(depth)]
    half = piece.shape[0] // 2
    from_behind, from_ahead = [piece], [piece]
    for _ in range(1, depth // 2):
        from_behind.append(lax.ppermute(from_behind[-1], "z", ahead))
        from_ahead.append(lax.ppermute(from_ahead[-1], "z", behind))
    far = (
        lax.ppermute(from_behind[-1][:half], "z", ahead),
        lax.ppermute(from_ahead[-1][half:], "z", behind),
    )
    return from_ahead + [far] + from_behind[:0:-1]


def sum_ring(slices, depth):
    assert depth == 8
    first, second = slices[4]
    half = first.shape[0]
    near = shift(slices[3], 1).astype(F32), shift(slices[5], -1).astype(F32)
    far = shift(first, 2).astype(F32), shift(second, -2).astype(F32)
    forward = slices[2].astype(F32) + near[0]
    backward = slices[6].astype(F32) + near[1]
    forward = jnp.concatenate([forward[:half] + far[0], forward[half:]], axis=0)
    backward = jnp.concatenate([backward[:half], backward[half:] + far[1]], axis=0)
    arrived = [
        shift(slices[1], 1),
        shift(slices[7], -1),
        shift(forward.astype(BF), 2),
        shift(backward.astype(BF), -2),
    ]
    return sum((part.astype(F32) for part in arrived), slices[0].astype(F32))


def sum_long_ring(slices, depth):
    ahead = [(i, (i + 1) % depth) for i in range(depth)]
    behind = [(i, (i + depth - 1) % depth) for i in range(depth)]

    def add(mine, arrived):
        return (mine.astype(F32) + arrived.astype(F32)).astype(BF)

    far = depth // 2
    first, second = slices[far]
    half = first.shape[0]
    forward = lax.ppermute(first, "z", ahead)
    backward = lax.ppermute(second, "z", behind)
    for offset in range(far - 1, 0, -1):
        mine, other = slices[offset], slices[depth - offset]
        if offset == far - 1:
            forward = jnp.concatenate([add(mine[:half], forward), mine[half:]], axis=0)
            backward = jnp.concatenate([other[:half], add(other[half:], backward)], axis=0)
        else:
            forward, backward = add(mine, forward), add(other, backward)
        forward = lax.ppermute(forward, "z", ahead)
        backward = lax.ppermute(backward, "z", behind)
    return slices[0].astype(F32) + forward.astype(F32) + backward.astype(F32)


def in_vmem(*operands):
    return [pltpu.with_memory_space_constraint(operand, pltpu.VMEM) for operand in operands]


def in_hbm(operand):
    return pltpu.with_memory_space_constraint(operand, pltpu.HBM)


def slice_shapes(depth, rows, width):
    shapes = [jax.ShapeDtypeStruct((rows, width), BF)] * (depth + 1)
    shapes[depth // 2] = shapes[depth // 2 + 1] = jax.ShapeDtypeStruct((rows // 2, width), BF)
    return shapes


def pair_far(slices):
    far = (len(slices) - 1) // 2
    return slices[:far] + [(slices[far], slices[far + 1])] + slices[far + 2 :]


def store_slices(group, outs, product_of):
    depth = len(outs) - 1
    far = depth // 2
    half, width = outs[far].shape
    for offset in range(depth):
        start = pl.multiple_of(lax.rem(group + offset, depth) * width, width)
        product = product_of(pl.ds(start, width)).astype(BF)
        if offset < far:
            outs[offset][...] = product
        elif offset > far:
            outs[offset + 1][...] = product
        else:
            outs[far][...] = product[:half]
            outs[far + 1][...] = product[half:]


def attention_kernel(
    group, queries, own_kv, other_kv, out_proj_hbm, out, out_proj, proj_sem
):
    rows = out_proj.shape[0] // PIECES
    proj_copies = [
        pltpu.make_async_copy(
            out_proj_hbm.at[pl.ds(piece * rows, rows)],
            out_proj.at[pl.ds(piece * rows, rows)],
            proj_sem.at[piece],
        )
        for piece in range(PIECES)
    ]
    for copy in proj_copies:
        copy.start()
    tokens, width = queries.shape
    heads = width // HD
    stacked = jnp.concatenate(
        [queries[:, head * HD : (head + 1) * HD] for head in range(heads)], axis=0
    )
    contract = (((1,), (1,)), ((), ()))
    scores = [
        lax.dot_general(stacked, kv[:, :HD], contract, preferred_element_type=F32)
        for kv in (own_kv, other_kv)
    ]
    top = jnp.maximum(*[jnp.max(part, axis=1, keepdims=True) for part in scores])
    weights = [jnp.exp((part - top) * HD ** (-0.5)) for part in scores]
    total = sum(jnp.sum(part, axis=1, keepdims=True) for part in weights)
    values = sum(
        jnp.dot(part.astype(BF), kv[:, HD:], preferred_element_type=F32)
        for part, kv in zip(weights, (own_kv, other_kv))
    )
    attended = (values / total).astype(BF)
    attended = jnp.concatenate(
        [attended[head * tokens : (head + 1) * tokens] for head in range(heads)], axis=1
    )
    for copy in proj_copies:
        copy.wait()
    depth = out_proj.shape[1] // SLICE
    for offset in range(depth):
        start = pl.multiple_of(lax.rem(group[0] + offset, depth) * SLICE, SLICE)
        product = jnp.dot(
            attended, out_proj[:, pl.ds(start, SLICE)], preferred_element_type=F32
        )
        out[:, offset * SLICE : (offset + 1) * SLICE] = product.astype(BF)


def attention_slices(group, queries, own_kv, other_kv, out_proj, depth):
    tokens, width = queries.shape
    total = pl.pallas_call(
        attention_kernel,
        out_shape=jax.ShapeDtypeStruct((tokens, out_proj.shape[1]), BF),
        in_specs=[pl.BlockSpec(memory_space=pltpu.SMEM)]
        + [pl.BlockSpec(memory_space=pltpu.VMEM)] * 3
        + [pl.BlockSpec(memory_space=pl.ANY)],
        out_specs=pl.BlockSpec(memory_space=pltpu.VMEM),
        scratch_shapes=[
            pltpu.VMEM(out_proj.shape, BF),
            pltpu.SemaphoreType.DMA((PIECES,)),
        ],
        compiler_params=pltpu.CompilerParams(vmem_limit_bytes=32 * 2**20),
        name="attention",
    )(group, *in_vmem(queries, own_kv, other_kv), in_hbm(out_proj))
    slices = [total[:, offset * SLICE : (offset + 1) * SLICE] for offset in range(depth)]
    far = slices[depth // 2]
    slices[depth // 2] = (far[: tokens // 2], far[tokens // 2 :])
    return slices


def dispatch_kernel(group, selector, gain, *refs):
    *pieces, out = refs
    far = (len(pieces) - 1) // 2
    whole = [piece[...].astype(F32) for piece in pieces]
    whole[far : far + 2] = [jnp.concatenate(whole[far : far + 2], axis=0)]
    depth = len(whole)
    width = whole[0].shape[1]
    square = sum(jnp.sum(piece * piece, axis=1, keepdims=True) for piece in whole)
    scale = lax.rsqrt(square / (depth * width) + 1e-06)
    for offset, piece in enumerate(whole):
        start = pl.multiple_of(lax.rem(group[0] + offset, depth) * width, width)
        columns = pl.ds(start, width)
        normed = (piece * scale * gain[:, columns]).astype(BF)
        rows = jnp.dot(selector[...], normed, preferred_element_type=F32).astype(BF)
        rows = rows.reshape(out.shape[0], out.shape[2], width)
        for copy in range(out.shape[1]):
            out[:, copy, :, columns] = rows


def dispatch_rows(group, selector, gain, pieces, experts, copies):
    far = len(pieces) // 2
    flat = pieces[:far] + list(pieces[far]) + pieces[far + 1 :]
    width = gain.shape[1]
    return pl.pallas_call(
        dispatch_kernel,
        out_shape=jax.ShapeDtypeStruct(
            (experts, copies, selector.shape[0] // experts, width), BF
        ),
        in_specs=[pl.BlockSpec(memory_space=pltpu.SMEM)]
        + [pl.BlockSpec(memory_space=pltpu.VMEM)] * (2 + len(flat)),
        out_specs=pl.BlockSpec(memory_space=pltpu.VMEM),
        compiler_params=pltpu.CompilerParams(vmem_limit_bytes=24 * 2**20),
        name="dispatch",
    )(group, *in_vmem(selector, gain, *flat))


def combine_kernel(group, weights, returned, *outs):
    store_slices(
        group[0],
        outs,
        lambda columns: jnp.dot(
            weights[...], returned[:, columns], preferred_element_type=F32
        ),
    )


def combine_slices(group, weights, returned, depth):
    shapes = slice_shapes(depth, weights.shape[0], returned.shape[1] // depth)
    slices = pl.pallas_call(
        combine_kernel,
        out_shape=shapes,
        in_specs=[pl.BlockSpec(memory_space=pltpu.SMEM)]
        + [pl.BlockSpec(memory_space=pltpu.VMEM)] * 2,
        out_specs=[pl.BlockSpec(memory_space=pltpu.VMEM)] * len(shapes),
        compiler_params=pltpu.CompilerParams(vmem_limit_bytes=16 * 2**20),
        name="combine",
    )(group, *in_vmem(weights, returned))
    return pair_far(list(slices))


def expert_kernel(
    rows, gate_a, up_a, down_a, gate_b, up_b, down_b, out,
    gates, ups, downs, totals, hidden, in_sem, down_sem,
):
    part = gate_a.shape[1]
    depth = gate_a.shape[0]
    width = depth // PIECES
    bounds = [depth * eighth // 8 for eighth in EIGHTHS]
    steps = len(bounds) - 1

    def in_copies(step):
        here = pl.ds(bounds[step], bounds[step + 1] - bounds[step])
        return [
            pltpu.make_async_copy(part_ref.at[here], store.at[which, here], in_sem.at[2 * which + kind, step])
            for which, pair in enumerate(((gate_a, up_a), (gate_b, up_b)))
            for kind, (part_ref, store) in enumerate(zip(pair, (gates, ups)))
        ]

    def down_copies():
        return [
            pltpu.make_async_copy(down, downs.at[pl.ds(which * part, part)], down_sem.at[which])
            for which, down in enumerate((down_a, down_b))
        ]

    def start(step):
        copies = in_copies(step) if step < steps else down_copies() if step == steps else []
        for copy in copies:
            copy.start()

    for step in range(AHEAD):
        start(step)
    for step in range(steps):
        start(step + AHEAD)
        for copy in in_copies(step):
            copy.wait()
        here = pl.ds(bounds[step], bounds[step + 1] - bounds[step])
        weights = jnp.concatenate(
            [gates[0, here], gates[1, here], ups[0, here], ups[1, here]], axis=1
        )
        product = jnp.dot(rows[:, here], weights, preferred_element_type=F32)
        if step:
            product += totals[...]
        if step < steps - 1:
            totals[...] = product
    gate_out, up_out = product[:, : 2 * part], product[:, 2 * part :]
    hidden[...] = (jax.nn.silu(gate_out) * up_out).astype(BF)
    for copy in down_copies():
        copy.wait()
    for piece in range(PIECES):
        columns = pl.ds(piece * width, width)
        out[:, columns] = jnp.dot(
            hidden[...], downs[:, columns], preferred_element_type=F32
        ).astype(BF)


def expert_partial(rows, *parts):
    count, depth = rows.shape
    part = parts[0].shape[1]
    return pl.pallas_call(
        expert_kernel,
        out_shape=pltpu.VMEM((count, depth), BF),
        in_specs=[pl.BlockSpec(memory_space=pltpu.VMEM)]
        + [pl.BlockSpec(memory_space=pl.ANY)] * len(parts),
        out_specs=pl.BlockSpec(memory_space=pltpu.VMEM),
        scratch_shapes=[
            pltpu.VMEM((2, depth, part), BF),
            pltpu.VMEM((2, depth, part), BF),
            pltpu.VMEM((2 * part, depth), BF),
            pltpu.VMEM((count, 4 * part), F32),
            pltpu.VMEM((count, 2 * part), BF),
            pltpu.SemaphoreType.DMA((4, len(EIGHTHS) - 1)),
            pltpu.SemaphoreType.DMA((2,)),
        ],
        compiler_params=pltpu.CompilerParams(vmem_limit_bytes=36 * 2**20),
        cost_estimate=pl.CostEstimate(
            flops=12 * count * depth * part,
            bytes_accessed=12 * depth * part + 4 * count * depth,
            transcendentals=2 * count * part,
        ),
        name="expert_partial",
    )(pltpu.with_memory_space_constraint(rows, pltpu.VMEM), *parts)


def shards(
    residual_in,
    queries,
    key_heads,
    value_heads,
    out_proj,
    norm_gain,
    expert_ids,
    route_weights,
    changed,
    cached_moe,
    gate_proj,
    up_proj,
    down_proj,
):
    plane = lax.axis_size("x") * lax.axis_size("y")
    depth = lax.axis_size("z")
    group_index = lax.axis_index("z")
    tokens = queries.shape[0]

    own_kv = gather_by_exchange(
        jnp.concatenate([key_heads, value_heads], axis=1), ("x", "y"), plane
    )
    own_kv = own_kv.reshape(-1, own_kv.shape[-1])
    other_kv = swap_cores(own_kv)

    other_parts = tuple(swap_cores(part[0]) for part in (gate_proj, up_proj, down_proj))

    capacity = 2 * tokens * TOP // (EXP_GROUP * depth)
    copies = plane // EXP_GROUP
    local_experts = jnp.arange(EXP_GROUP, dtype=jnp.int32) + group_index * EXP_GROUP
    matches = expert_ids[:, :, None] == local_experts[None, None, :]
    member = jnp.any(matches, axis=1)
    token_weight = jnp.sum(
        jnp.where(matches, route_weights[:, :, None], jnp.zeros((), BF)), axis=1
    )
    rank = jnp.cumsum(member.astype(jnp.int32), axis=0) - 1
    live_rows = member & (changed[:, None] == 1)
    slot_range = jnp.arange(capacity, dtype=jnp.int32)
    select_hit = live_rows.T[:, None, :] & (rank.T[:, None, :] == slot_range[None, :, None])
    selector = select_hit.astype(BF)
    weighted_select = selector * token_weight.T[:, None, :]
    weighted_select = jnp.repeat(weighted_select, copies, axis=0)
    weighted_select = weighted_select.reshape(-1, tokens).T
    group = group_index.astype(jnp.int32).reshape(1)
    slices = attention_slices(group, queries, own_kv, other_kv, out_proj, depth)
    slices, selector, weighted_select = lax.optimization_barrier(
        (slices, selector, weighted_select)
    )
    attn_share = sum_long_ring(slices, depth)
    mixed_local = (residual_in.astype(F32) + attn_share).astype(BF)
    mixed_pieces = gather_ring(mixed_local, depth)

    outgoing = dispatch_rows(
        group,
        selector.reshape(-1, tokens),
        norm_gain.reshape(1, -1),
        mixed_pieces,
        EXP_GROUP,
        copies,
    )
    outgoing = outgoing.reshape(plane, capacity, -1)
    own_parts = (gate_proj[0], up_proj[0], down_proj[0])
    outgoing, own_parts, other_parts, weighted_select = lax.optimization_barrier(
        (outgoing, own_parts, other_parts, weighted_select)
    )
    arrived = lax.all_to_all(outgoing, ("x", "y"), split_axis=0, concat_axis=0, tiled=True)
    rows = arrived.reshape(-1, arrived.shape[-1])

    partial_out = expert_partial(rows, *own_parts, *other_parts)
    returned = lax.all_to_all(
        partial_out.reshape(arrived.shape), ("x", "y"), split_axis=0, concat_axis=0, tiled=True
    )
    moe_share = sum_ring(
        combine_slices(group, weighted_select, returned.reshape(rows.shape), depth), depth
    )
    moe_value = jnp.where(changed[:, None] == 1, moe_share, cached_moe.astype(F32))
    return (mixed_local.astype(F32) + moe_value).astype(BF)


def solution(mesh):
    cores = 2
    side = int(round((mesh.shape["seq"] // cores) ** 0.5))
    split_mesh = Mesh(
        mesh.devices.reshape(side, side, cores, mesh.shape["exp"]), ("x", "y", "c", "z")
    )
    seq = ("x", "y", "c")
    in_specs = (
        P(seq, "z"),
        P(seq, "z"),
        P(seq, "z"),
        P(seq, "z"),
        P("z", None),
        P(),
        P(seq, None),
        P(seq, None),
        P(seq),
        P(seq, "z"),
        P(("z",) + seq, None, None),
        P(("z",) + seq, None, None),
        P(("z",) + seq, None, None),
    )
    return jax.shard_map(
        shards, mesh=split_mesh, in_specs=in_specs, out_specs=P(seq, "z"), check_vma=False
    )
```
